256 devices in a mesh: tm: 8 (over z_lo, x), rows: 32 (over z_hi, y, core).
Axes of the slice: x: 4, y: 4, z: 8 (z_hi: 4, z_lo: 2; z = z_hi * 2 + z_lo), core: 2. Of those that a mesh axis runs over, the one named last changes fastest.
Arguments:
- noisy_frames: bfloat16 [3, 128, 256, 128], P(None, 'tm', 'rows'), may hold values from -6 to 6
- base_queue: bfloat16 [128, 3, 32, 16], P('tm', None, 'rows'), may hold values from -6 to 6
- frame_slot: int32 [128], replicated, may hold values from 0 to 127, each once
- blend_weight: int32 [128, 2], P('tm'), may hold values from 1 to 8
- weight_in: bfloat16 [3, 3, 6, 128], replicated, may hold values from -0.875 to 0.875
- bias_in: float32 [128], replicated, may hold values from -3 to 3
- gain_mid: float32 [128], replicated, may hold values from 0.1 to 1.9
- weight_mid: bfloat16 [3, 3, 128, 128], replicated, may hold values from -0.1875 to 0.1875
- time_mix: bfloat16 [128, 16, 16], replicated, may hold values from -1.5 to 1.5
- weight_out: bfloat16 [128, 3], replicated, may hold values from -0.5 to 0.5
- bias_out: float32 [3], replicated, may hold values from -3 to 3
Outputs:
- blended: float32 [3, 128, 256, 128], P(None, 'tm', 'rows')
The draws below stay inside these ranges and needn't reach their ends.
Inputs may be any that keep to these rules, and one draw needn't show every extreme that they name: `frame_slot`: every queue slot holds exactly one frame.
All inputs are finite; a program needn't handle non-finite values.
Results may differ from the reference program's by a relative error of at most 0.0038.
Values may be sent and summed in bfloat16 or wider, within the bound.
No kernel may reach another device: no remote copies, remote signals or barrier semaphores. Data moves between devices by JAX's collectives and lax.ppermute only.
A program may use at most 128 MiB of HBM per device.

```python
import jax
import jax.numpy as jnp
from jax import lax

CHANNELS = 128
WINDOW = 16
UPSCALE = 8
COLS = 128
FRAMES = 128
HEIGHT = 256
BASE_ROWS = 32
BASE_COLS = 16
N_TM = 8


def with_ends(values, own_key, low, high):
    shape = values.shape
    place = [jax.random.randint(jax.random.fold_in(own_key, axis), (), 0, shape[axis]) for axis in range(len(shape))]
    values = values.at[tuple(place)].set(low)
    longest = shape.index(max(shape))
    place[longest] = (place[longest] + 1) % shape[longest]
    return values.at[tuple(place)].set(high)


def block_scale(rng, dims, pieces, least, top_value):
    def one(position, blocks):
        draws = jax.random.uniform(jax.random.fold_in(jax.random.fold_in(rng, 6), position), (blocks,), jnp.float32, least / len(pieces), top_value / len(pieces))
        return jnp.repeat(jnp.exp(draws), dims[position] // blocks).reshape((-1,) + (1,) * (len(dims) - position - 1))

    gain = one(*pieces[0])
    for cut in pieces[1:]:
        gain = gain * one(*cut)
    return gain


def scatter_about(key, extent, scale, reach, pieces=(), kind=jnp.bfloat16):
    level = block_scale(key, extent, pieces, -0.22, 0.18) if pieces else 1.0
    values = jax.random.normal(key, extent, jnp.float32) * scale * level
    return jnp.minimum(jnp.maximum(values, -reach), reach).astype(kind)


def setup_inputs(seed: int = 0) -> dict:
    splits = jax.random.split(jax.random.key(seed), 12)
    return {
        "noisy_frames": scatter_about(splits[0], (3, FRAMES, HEIGHT, COLS), 1.0, 6.0, ((1, 8), (2, 32))),
        "base_queue": scatter_about(splits[1], (FRAMES, 3, BASE_ROWS, BASE_COLS), 1.0, 6.0, ((0, 8), (2, 32))),
        "frame_slot": jax.random.permutation(splits[2], FRAMES).astype(jnp.int32),
        "blend_weight": with_ends(jax.random.randint(splits[3], (FRAMES, 2), 1, 9), jax.random.fold_in(splits[3], 1), 1, 8).astype(jnp.int32),
        "weight_in": scatter_about(splits[4], (3, 3, 6, CHANNELS), 54 ** -0.5, 0.875),
        "bias_in": scatter_about(splits[5], (CHANNELS,), 0.5, 3.0, (), jnp.float32),
        "gain_mid": jnp.clip(1.0 + 0.18 * jax.random.normal(splits[6], (CHANNELS,), jnp.float32), 0.1, 1.9),
        "weight_mid": scatter_about(splits[7], (3, 3, CHANNELS, CHANNELS), (9 * CHANNELS) ** -0.5, 0.1875),
        "time_mix": scatter_about(splits[8], (CHANNELS, WINDOW, WINDOW), WINDOW ** -0.5, 1.5),
        "weight_out": scatter_about(splits[9], (CHANNELS, 3), CHANNELS ** -0.5, 0.5),
        "bias_out": scatter_about(splits[10], (3,), 0.5, 3.0, (), jnp.float32),
    }


def shifted_conv(source, weight):
    return lax.conv_general_dilated(source.astype(jnp.float32), weight.astype(jnp.float32), (1, 1), ((1, 1), (1, 1)), dimension_numbers=('CNHW', 'HWIO', 'CNHW'), precision=lax.Precision.HIGHEST)

def window_pred(frames_in, weight_in, bias_in, gain_mid, weight_mid, time_mix, weight_out, bias_out):
    hidden = shifted_conv(frames_in, weight_in) + bias_in[:, None, None, None]
    scale = lax.rsqrt(lax.optimization_barrier(jnp.mean(hidden * hidden, axis=0, keepdims=True)) + 1e-06)
    active = jax.nn.silu(hidden * scale * gain_mid[:, None, None, None]).astype(jnp.bfloat16)
    spatial = shifted_conv(active, weight_mid).astype(jnp.bfloat16)
    spatial_wide = spatial.astype(jnp.float32)
    mixed = jnp.einsum('cfg,cgrw->cfrw', time_mix.astype(jnp.float32), spatial_wide)
    outer = jax.nn.silu(spatial_wide + mixed).astype(jnp.bfloat16)
    return jnp.einsum('co,cfrw->ofrw', weight_out.astype(jnp.float32), outer.astype(jnp.float32)) + bias_out[:, None, None, None]

def reference(noisy_frames, base_queue, frame_slot, blend_weight, weight_in, bias_in, gain_mid, weight_mid, time_mix, weight_out, bias_out):
    chosen = jnp.transpose(jnp.take(base_queue, frame_slot, axis=0), (1, 0, 2, 3))
    lifted = jnp.repeat(jnp.repeat(chosen, UPSCALE, axis=2), UPSCALE, axis=3)
    inputs = jnp.concatenate([noisy_frames, lifted], axis=0)
    half = WINDOW // 2
    count = 2 * N_TM - 1
    starts = jnp.arange(count, dtype=jnp.int32) * half

    def one_window(start):
        frames_in = lax.dynamic_slice_in_dim(inputs, start, WINDOW, 1)
        return window_pred(frames_in, weight_in, bias_in, gain_mid, weight_mid, time_mix, weight_out, bias_out)
    preds = lax.map(one_window, starts)
    blocks = count + 1
    zero_block = jnp.zeros_like(preds[:1, :, :half])
    lead_all = jnp.concatenate([preds[:, :, :half], zero_block], axis=0)
    trail_all = jnp.concatenate([zero_block, preds[:, :, half:]], axis=0)
    weights = blend_weight.astype(jnp.float32).reshape(blocks, half, 2)
    block_ids = jnp.arange(blocks, dtype=jnp.int32)
    lead_valid = (block_ids < count).astype(jnp.float32)
    trail_valid = (block_ids >= 1).astype(jnp.float32)
    lead_w = weights[:, :, 0] * lead_valid[:, None]
    trail_w = weights[:, :, 1] * trail_valid[:, None]
    numer = lead_w[:, None, :, None, None] * lead_all + trail_w[:, None, :, None, None] * trail_all
    denom = (lead_w + trail_w)[:, None, :, None, None]
    result = numer / denom
    return jnp.transpose(result, (1, 0, 2, 3, 4)).reshape(3, FRAMES, HEIGHT, COLS)
```

```python
import functools

import jax
import jax.numpy as jnp
import numpy as np
from jax import lax
from jax.experimental import pallas as pl
from jax.experimental.pallas import tpu as pltpu
from jax.sharding import PartitionSpec as P

BF16 = jnp.bfloat16
F32 = jnp.float32
NT = (((1,), (1,)), ((), ()))
VMEM = pl.BlockSpec(memory_space=pltpu.VMEM)
SMEM = pl.BlockSpec(memory_space=pltpu.SMEM)
PARAMS = pltpu.CompilerParams(vmem_limit_bytes=56 * 2**20)


def column_of_pixel():
    p = np.arange(128)
    return (p % 16) * 8 + p // 16


def shift_matrix():
    m = np.zeros((128, 3, 128), np.float32)
    col = column_of_pixel()
    for dv in range(3):
        for p in range(128):
            c = col[p] + dv - 1
            if 0 <= c < 128:
                m[p, dv, c] = 1
    return m.reshape(128, 384)


def unorder_matrix():
    m = np.zeros((128, 128), np.float32)
    m[np.arange(128), column_of_pixel()] = 1
    return m


def widen_matrix():
    m = np.zeros((128, 3, 128), np.float32)
    for br in range(3):
        for c in range(128):
            m[br * 16 + c // 8, br, c] = 1
    return m.reshape(128, 384)


def tap_matrix():
    m = np.zeros((5, 2, 256, 64), np.float32)
    for q in range(5):
        for e in range(2):
            for dr in range(3):
                row = 2 * q + e - 2 + dr
                for dv in range(3):
                    for ch in range(6):
                        tap = (dr * 3 + dv) * 6 + ch
                        if ch < 3:
                            if 0 <= row < 8:
                                k = ch * 8 + row
                            else:
                                k = 24 + ch * 8 + (row + 2 if row < 0 else row - 6)
                            m[q, e, dv * 80 + k, tap] += 1
                        else:
                            br = 0 if row < 0 else (1 if row < 8 else 2)
                            m[q, e, dv * 80 + 48 + br * 8 + ch - 3, tap] += 1
                            m[q, e, dv * 80 + 48 + br * 8 + ch, tap] += 1
    return m.reshape(10, 256, 64)


def iota(shape, dim):
    return lax.broadcasted_iota(jnp.int32, shape, dim)


def prepare_kernel(taps, win, bias, wmid, mix, wout, w_in, w_mid, w_mix, w_out):
    k = iota((256, 128), 0)
    low = (k % 80 >= 48) & (k % 80 < 72) & (k % 8 >= 3) & (k % 8 < 6) & (k < 240)
    b = bias[...]
    b0 = b.astype(BF16).astype(F32)
    b1 = (b - b0).astype(BF16).astype(F32)
    b2 = b - b0 - b1
    for q in range(5):
        for e in range(2):
            v = jnp.dot(taps[2 * q + e], win[...], preferred_element_type=F32)
            v = jnp.where(low, v - v.astype(BF16).astype(F32), v)
            v = jnp.where(k == 152, b0, jnp.where(k == 153, b1, jnp.where(k == 154, b2, v)))
            w_in[q, :, e * 128 : (e + 1) * 128] = v.astype(BF16)
    w_mid[...] = jnp.zeros_like(w_mid)
    for dr in range(3):
        for dv in range(3):
            t = wmid[dr * 3 + dv].T
            for e in range(2):
                tap = (dr + e) * 3 + dv
                w_mid[e * 128 : (e + 1) * 128, tap * 128 : (tap + 1) * 128] = t
    r = iota((256, 256), 0)
    c = iota((256, 256), 1)
    reorder = ((r // 16 == c % 16) & (r % 16 == c // 16)).astype(BF16)
    over = (iota((16, 256), 0) == iota((16, 256), 1) // 16).astype(BF16)
    same = r % 16 == c % 16
    for g in range(8):
        t = jnp.dot(reorder, mix[g * 256 : (g + 1) * 256, :], preferred_element_type=F32)
        t = jnp.dot(t.astype(BF16), over, preferred_element_type=F32)
        w_mix[g] = jnp.where(same, t, 0.0).astype(BF16)
    own = iota((16, 256), 0) == iota((16, 256), 1) // 16
    for g in range(8):
        pick = (iota((128, 256), 0) == g * 16 + iota((128, 256), 1) % 16).astype(BF16)
        t = jnp.dot(wout[...], pick, preferred_element_type=F32)
        for o in range(3):
            w_out[g, o * 16 : (o + 1) * 16, :] = jnp.where(own, t[o : o + 1, :], 0.0).astype(BF16)


def lift(base, hot, widen, lifted):
    chosen = jnp.dot(hot[...], base[...], preferred_element_type=F32).astype(BF16)
    lifted[...] = jnp.dot(chosen, widen[...], preferred_element_type=F32)


def activate(own, rim, first, lifted, lift_first, shift, w_in, mean, gain, depth, act):
    ones = jnp.ones((8, 128), F32)
    zero = jnp.zeros((80, 128), BF16)
    end = jnp.zeros((16, 384), BF16)
    for f in range(8):
        tiles = [own[ch, first + f].astype(F32) for ch in range(3)]
        tiles += [rim[ch, first + f].astype(F32) for ch in range(3)]
        at = (lift_first + f) * 8
        tiles += [lifted[at : at + 8, br * 128 : (br + 1) * 128] for br in range(3)]
        x = jnp.concatenate(tiles + [ones], axis=0).astype(BF16)
        x = jnp.concatenate(
            [
                jnp.concatenate([x, zero, zero], axis=1),
                jnp.concatenate([zero, x, zero], axis=1),
                jnp.concatenate([zero, zero, x], axis=1),
                end,
            ],
            axis=0,
        )
        d = lax.dot_general(shift[...], x, NT, preferred_element_type=F32)
        depth[f * 128 : (f + 1) * 128, :] = d.astype(BF16)
    s = iota((16, 256), 0)
    for q in range(5):
        h = jnp.dot(depth[...], w_in[q], preferred_element_type=F32)
        ss = jnp.dot((h * h).astype(BF16), mean[...], preferred_element_type=F32)
        u = h * lax.rsqrt(ss + 1e-6) * gain[q : q + 1, :]
        a = (u * jnp.tanh(u) + u).reshape(8, 128, 256)
        body = a.astype(BF16).reshape(8, 8, 16, 256)
        for e in range(2):
            act[:, 2 * q + e, 1:9] = body[:, :, :, e * 128 : (e + 1) * 128]
        for f in range(8):
            left = jnp.where(s == 0, 0.0, pltpu.roll(a[f, 112:128], 1, 0)).astype(BF16)
            right = jnp.where(s == 15, 0.0, pltpu.roll(a[f, 0:16], 15, 0)).astype(BF16)
            for e in range(2):
                act[f, 2 * q + e, 0] = left[:, e * 128 : (e + 1) * 128]
                act[f, 2 * q + e, 9] = right[:, e * 128 : (e + 1) * 128]


def convolve(act, w_mid, spatial, first):
    @pl.loop(0, 4)
    def _(pair):
        for i in range(4):
            frames = []
            for b in range(2):
                taps = [
                    act[pair * 2 + b, 2 * i + dr, dv : dv + 8].reshape(128, 128)
                    for dr in range(4)
                    for dv in range(3)
                ]
                frames.append(jnp.concatenate(taps, axis=1))
            x = jnp.concatenate(frames, axis=0)
            y = lax.dot_general(w_mid[...], x, NT, preferred_element_type=F32).astype(BF16)
            for b in range(2):
                for e in range(2):
                    spatial[i, first + pair * 2 + b, :, e * 128 : (e + 1) * 128] = y[
                        e * 128 : (e + 1) * 128, b * 128 : (b + 1) * 128
                    ]


def predict(spatial, w_mix, w_out, bias_out, total):
    @pl.loop(0, 4)
    def _(i):
        acc = None
        for g in range(8):
            x = spatial[i, :, g * 16 : (g + 1) * 16, :].reshape(256, 256)
            h = 0.5 * (jnp.dot(w_mix[g], x, preferred_element_type=F32) + x.astype(F32))
            outer = (h * jnp.tanh(h) + h).astype(BF16)
            p = jnp.dot(w_out[g], outer, preferred_element_type=F32)
            acc = p if acc is None else acc + p
        for o in range(3):
            part = acc[o * 16 : (o + 1) * 16, :] + bias_out[0, o]
            for e in range(2):
                total[2 * i + e, o * 16 : (o + 1) * 16, :] = part[:, e * 128 : (e + 1) * 128]


def unorder(total, order, rows):
    x = total[...].reshape(384, 128)
    x0 = x.astype(BF16)
    r = x - x0.astype(F32)
    x1 = r.astype(BF16)
    x2 = (r - x1.astype(F32)).astype(BF16)
    y = [jnp.dot(part, order[...], preferred_element_type=F32) for part in (x0, x1, x2)]
    rows[...] = y[0] + (y[1] + y[2])


def picture(rows, o, f):
    return rows[pl.ds(o * 16 + f, 8, stride=48), :]


def late_kernel(
    own, ahead, rim, rim_ahead, base, hot, widen, shift, w_in, w_mid, w_mix, w_out, mean, order,
    gain, bias_out, send, near, kept, lifted, depth, act, spatial, total, rows,
):
    lift(base, hot, widen, lifted)
    activate(own, rim, 8, lifted, 0, shift, w_in, mean, gain, depth, act)
    convolve(act, w_mid, spatial, 0)
    activate(ahead, rim_ahead, 0, lifted, 8, shift, w_in, mean, gain, depth, act)
    convolve(act, w_mid, spatial, 8)
    kept[...] = spatial[:, 0:8]
    predict(spatial, w_mix, w_out, bias_out, total)
    unorder(total, order, rows)
    for o in range(3):
        for f in range(8):
            near[o, f] = picture(rows, o, f)
            send[o, f] = picture(rows, o, f + 8).astype(BF16)


def early_kernel(
    own, rim, base, hot, widen, shift, w_in, w_mid, w_mix, w_out, mean, order,
    gain, bias_out, near, kept, share, out, lifted, depth, act, spatial, total, rows,
):
    lift(base, hot, widen, lifted)
    activate(own, rim, 0, lifted, 0, shift, w_in, mean, gain, depth, act)
    spatial[:, 8:16] = kept[...]
    convolve(act, w_mid, spatial, 0)
    predict(spatial, w_mix, w_out, bias_out, total)
    unorder(total, order, rows)
    for o in range(3):
        for f in range(8):
            out[o, f] = picture(rows, o, f) * share[0, f]
            out[o, f + 8] = picture(rows, o, f + 8) * share[1, f + 8] + near[o, f] * share[0, f + 8]


def scratch(frames):
    return [
        pltpu.VMEM((frames * 8, 384), F32),
        pltpu.VMEM((1024, 256), BF16),
        pltpu.VMEM((8, 10, 10, 16, 128), BF16),
        pltpu.VMEM((4, 16, 128, 256), BF16),
        pltpu.VMEM((8, 48, 128), F32),
        pltpu.VMEM((384, 128), F32),
    ]


def shape(dims, kind):
    return jax.ShapeDtypeStruct(dims, kind)


def prepare(weight_in, bias_in, weight_mid, time_mix, weight_out):
    win = jnp.pad(weight_in.reshape(54, 128), ((0, 10), (0, 0)))
    wout = jnp.pad(weight_out.T, ((0, 13), (0, 0)))
    return pl.pallas_call(
        prepare_kernel,
        out_shape=(
            shape((5, 256, 256), BF16),
            shape((256, 1536), BF16),
            shape((8, 256, 256), BF16),
            shape((8, 48, 256), BF16),
        ),
        in_specs=[VMEM] * 6,
        out_specs=(VMEM,) * 4,
        compiler_params=PARAMS,
        cost_estimate=pl.CostEstimate(flops=10**9, bytes_accessed=3 * 10**6, transcendentals=0),
        name="prepare",
    )(
        jnp.asarray(tap_matrix(), BF16),
        win,
        bias_in.reshape(1, 128),
        weight_mid.reshape(9, 128, 128),
        time_mix.reshape(2048, 16),
        wout,
    )


def body(
    noisy_frames, base_queue, frame_slot, blend_weight, weight_in, bias_in, gain_mid, weight_mid,
    time_mix, weight_out, bias_out,
):
    t = lax.axis_index("tm")
    r = lax.axis_index("rows")
    n_t = lax.axis_size("tm")
    n_r = lax.axis_size("rows")
    down = [(i, i + 1) for i in range(n_r - 1)]
    up = [(i + 1, i) for i in range(n_r - 1)]
    back = [(i + 1, i) for i in range(n_t - 1)]
    forth = [(i, i + 1) for i in range(n_t - 1)]

    base = jnp.transpose(base_queue[:, :, 0, :], (1, 0, 2))
    wide = jnp.pad(base, ((0, 0), (0, 0), (0, 112)))[:, :, None, :]
    ahead = lax.ppermute(noisy_frames[:, :8], "tm", back)
    low = lax.ppermute(jnp.concatenate([noisy_frames[:, :, 6:], wide], axis=2), "rows", down)
    high = lax.ppermute(jnp.concatenate([noisy_frames[:, :, :2], wide], axis=2), "rows", up)
    rim = jnp.concatenate(
        [low[:, :, :2], high[:, :, :2], jnp.zeros((3, 16, 4, 128), BF16)], axis=2
    )
    rim_ahead = lax.ppermute(rim[:, :8], "tm", back)
    three = jnp.concatenate([low[:, :, 2, :16], base, high[:, :, 2, :16]], axis=2)
    three = jnp.pad(three.reshape(48, 48), ((0, 0), (0, 80)))
    queue = lax.all_to_all(
        jnp.broadcast_to(three[None], (n_t, 48, 128)), "tm", 0, 0, tiled=True
    ).reshape(384, 128)

    slots = jnp.take(frame_slot, jnp.minimum(t * 16 + jnp.arange(24), 127))
    j = jnp.arange(8)
    place = (slots[:, None] // 16) * 48 + (j[None, :] % 3) * 16 + slots[:, None] % 16
    place = jnp.where(j[None, :] < 6, place, -1).reshape(192, 1)
    hot = (place == jnp.arange(384)[None, :]).astype(BF16)

    w_in, w_mid, w_mix, w_out = prepare(weight_in, bias_in, weight_mid, time_mix, weight_out)
    half_gain = jnp.tile(0.5 * gain_mid, 10).reshape(10, 128)
    inside = jnp.ones((10,), F32).at[0].set((r > 0).astype(F32)).at[9].set((r < n_r - 1).astype(F32))
    gain = (half_gain * inside[:, None]).reshape(5, 256)
    mean = jnp.asarray(np.kron(np.eye(2), np.full((128, 128), 1 / 128)), BF16)
    order = jnp.asarray(unorder_matrix(), BF16)
    shift = jnp.asarray(shift_matrix(), BF16)
    widen = jnp.asarray(widen_matrix(), BF16)
    b_out = bias_out.reshape(1, 3)

    w = blend_weight.astype(F32)
    late = jnp.arange(16) >= 8
    lead = w[:, 0] * jnp.where(late, (t < n_t - 1).astype(F32), 1.0)
    trail = w[:, 1] * jnp.where(late, 1.0, (t > 0).astype(F32))
    share = jnp.stack([lead, trail]) / (lead + trail)[None]
    wide_share = jnp.broadcast_to(share[:, :, None, None], (2, 16, 1, 128))

    send, near, kept = pl.pallas_call(
        late_kernel,
        out_shape=(
            shape((3, 8, 8, 128), BF16),
            shape((3, 8, 8, 128), F32),
            shape((4, 8, 128, 256), BF16),
        ),
        in_specs=[VMEM] * 15 + [SMEM],
        out_specs=(VMEM,) * 3,
        scratch_shapes=scratch(16),
        compiler_params=PARAMS,
        cost_estimate=pl.CostEstimate(flops=10**10, bytes_accessed=10**7, transcendentals=0),
        name="late",
    )(
        noisy_frames, ahead, rim, rim_ahead, queue, hot[64:], widen, shift, w_in, w_mid, w_mix,
        w_out, mean, order, gain, b_out,
    )
    arrived = lax.ppermute(send, "tm", forth)
    mine = pl.pallas_call(
        early_kernel,
        out_shape=shape((3, 16, 8, 128), F32),
        in_specs=[VMEM] * 13 + [SMEM] + [VMEM] * 3,
        out_specs=VMEM,
        scratch_shapes=scratch(8),
        compiler_params=PARAMS,
        cost_estimate=pl.CostEstimate(flops=10**10, bytes_accessed=10**7, transcendentals=0),
        name="early",
    )(
        noisy_frames, rim, queue, hot[:64], widen, shift, w_in, w_mid, w_mix, w_out, mean, order,
        gain, b_out, near, kept, wide_share,
    )
    early = mine[:, :8] + share[1, None, :8, None, None] * arrived.astype(F32)
    return jnp.concatenate([early, mine[:, 8:]], axis=1)


def solution(mesh):
    return jax.shard_map(
        body,
        mesh=mesh,
        in_specs=(
            P(None, "tm", "rows", None),
            P("tm", None, "rows", None),
            P(),
            P("tm", None),
            P(),
            P(),
            P(),
            P(),
            P(),
            P(),
            P(),
        ),
        out_specs=P(None, "tm", "rows", None),
        check_vma=False,
    )
```

```python
import functools

import jax
import jax.numpy as jnp
import numpy as np
from jax import lax
from jax.experimental import pallas as pl
from jax.experimental.pallas import tpu as pltpu
from jax.sharding import PartitionSpec as P

BF16 = jnp.bfloat16
F32 = jnp.float32
NT = (((1,), (1,)), ((), ()))
VMEM = pl.BlockSpec(memory_space=pltpu.VMEM)
HBM = pl.BlockSpec(memory_space=pltpu.HBM)
SMEM = pl.BlockSpec(memory_space=pltpu.SMEM)
PARAMS = pltpu.CompilerParams(vmem_limit_bytes=24 * 2**20)


def tap_matrix():
    m = np.zeros((5, 2, 256, 72), np.float32)
    for q in range(5):
        for e in range(2):
            for dr in range(3):
                row = 2 * q + e - 2 + dr
                for dv in range(3):
                    for ch in range(6):
                        tap = (dr * 3 + dv) * 8 + ch
                        if ch < 3:
                            if 0 <= row < 8:
                                k = ch * 8 + row
                            else:
                                k = 24 + ch * 8 + (row + 2 if row < 0 else row - 6)
                            m[q, e, dv * 80 + k, tap] += 1
                        else:
                            br = 0 if row < 0 else (1 if row < 8 else 2)
                            m[q, e, dv * 80 + 48 + br * 8 + ch - 3, tap] += 1
                            m[q, e, dv * 80 + 48 + br * 8 + ch, tap] += 1
    return m.reshape(10, 256, 72)


def spread_matrix():
    m = np.zeros((496, 256), np.float32)
    m[240 + np.arange(256) // 16, np.arange(256)] = 1
    return m


def iota(shape, dim):
    return lax.broadcasted_iota(jnp.int32, shape, dim)


def fetch(sources, targets, sems):
    copies = [
        pltpu.make_async_copy(source, target, sems.at[i])
        for i, (source, target) in enumerate(zip(sources, targets))
    ]
    for copy in copies:
        copy.start()
    for copy in copies:
        copy.wait()


def pack_kernel(own_hbm, queue_hbm, to_below, to_above, base, own, slots, queue, sems):
    fetch([own_hbm, queue_hbm], [own, queue], sems)
    x = pltpu.roll(own[...].astype(F32).reshape(48, 8, 128), 2, 1)
    row = iota((48, 8, 128), 1)
    put = (iota((16, 384), 0) == iota((16, 384), 1) % 128 - iota((16, 384), 1) // 128 * 16).astype(BF16)
    placed = jnp.dot(queue[...].reshape(48, 16), put, preferred_element_type=F32)
    slots[...] = jnp.zeros_like(slots)
    slots[pl.ds(4, 48, stride=8), :] = placed[:, :128]
    y = jnp.where(row < 2, x, slots[...].reshape(48, 8, 128))
    to_below[...] = y.astype(BF16).reshape(3, 16, 8, 128)
    slots[pl.ds(4, 48, stride=8), :] = jnp.zeros((48, 128), F32)
    slots[pl.ds(5, 48, stride=8), :] = placed[:, 256:]
    y = jnp.where((row >= 2) & (row < 4), x, slots[...].reshape(48, 8, 128))
    to_above[...] = y.astype(BF16).reshape(3, 16, 8, 128)
    base[...] = placed[:, 128:256]


def middle_kernel(
    blend_hbm, own, from_above, from_below, base, maps, rim, ask, back, both, blend, sems
):
    copy = pltpu.make_async_copy(blend_hbm, blend, sems.at[0])
    copy.start()
    x = from_above[...].astype(F32) + from_below[...].astype(F32)
    rim[...] = x.astype(BF16)
    both[...] = x.reshape(384, 128)
    three = both[pl.ds(4, 48, stride=8), :] + both[pl.ds(5, 48, stride=8), :] + base[...]
    three = three.astype(BF16)
    for i in range(ask.shape[0]):
        ask[i] = three
    copy.wait()
    row = iota((8, 128), 0)
    for ch in range(3):
        for f in range(8):
            y = x[ch, f]
            y = jnp.where(row == 6, blend[0, f].astype(F32), y)
            y = jnp.where(row == 7, blend[1, f].astype(F32), y)
            both_rows = jnp.concatenate([own[ch, f].astype(F32), y], axis=0)
            back[ch, f] = both_rows.astype(BF16)


def prepare_kernel(*refs):
    sources, (w_in, w_mid, w_mix, w_out, maps), targets = refs[:7], refs[7:12], refs[12:19]
    fetch(sources, targets, refs[19])
    taps, win, bias, wmid, mix, wout, over = targets
    col = iota((128, 384), 0)
    lane = iota((128, 384), 1)
    pixel = lane & 127
    maps[:, 0:384] = (col == (pixel & 15) * 8 + (pixel >> 4) + (lane >> 7) - 1).astype(BF16)
    maps[:, 384:768] = (col == (lane >> 7) * 16 + (pixel >> 3)).astype(BF16)
    col = iota((128, 128), 0)
    maps[:, 768:896] = (iota((128, 128), 1) == (col & 15) * 8 + (col >> 4)).astype(BF16)
    k = iota((256, 128), 0)
    low = (k % 80 >= 48) & (k % 80 < 72) & (k % 8 >= 3) & (k % 8 < 6) & (k < 240)
    b = bias[...]
    b0 = b.astype(BF16).astype(F32)
    b1 = (b - b0).astype(BF16).astype(F32)
    b2 = b - b0 - b1
    pad = jnp.zeros((2, 128), F32)
    w = [jnp.concatenate([win[i].astype(F32), pad], axis=0) for i in range(9)]
    w = jnp.concatenate(w, axis=0).astype(BF16)
    for q in range(5):
        for e in range(2):
            v = jnp.dot(taps[2 * q + e], w, preferred_element_type=F32)
            v = jnp.where(low, v - v.astype(BF16).astype(F32), v)
            v = jnp.where(k == 152, b0, jnp.where(k == 153, b1, jnp.where(k == 154, b2, v)))
            w_in[q, :, e * 128 : (e + 1) * 128] = v.astype(BF16)
    none = jnp.zeros((128, 384), BF16)
    w_mid[0:128, 1152:1536] = none
    w_mid[128:256, 0:384] = none
    for dr in range(3):
        for dv in range(3):
            t = wmid[dr * 3 + dv].T
            for e in range(2):
                tap = (dr + e) * 3 + dv
                w_mid[e * 128 : (e + 1) * 128, tap * 128 : (tap + 1) * 128] = t
    flat = mix[...].reshape(256, 128)
    flat = jnp.concatenate([flat[:128].T, flat[128:].T], axis=1)
    same = iota((128, 256), 0) % 16 == iota((128, 256), 1) % 16
    for p in range(16):
        t = jnp.dot(flat, over[240 - 16 * p : 496 - 16 * p, :], preferred_element_type=F32)
        t = jnp.where(same, t, 0.0).astype(BF16)
        for g in range(8):
            w_mix[g, p * 16 : (p + 1) * 16, :] = t[g * 16 : (g + 1) * 16, :]
    own = iota((16, 256), 0) == iota((16, 256), 1) // 16
    wo = jnp.concatenate([wout[...].astype(F32), jnp.zeros((5, 128), F32)], axis=0).astype(BF16)
    for g in range(8):
        pick = (iota((128, 256), 0) == g * 16 + iota((128, 256), 1) % 16).astype(BF16)
        t = jnp.dot(wo, pick, preferred_element_type=F32)
        for o in range(3):
            w_out[g, o * 16 : (o + 1) * 16, :] = jnp.where(own, t[o : o + 1, :], 0.0).astype(BF16)


def lift(frame_slot, queue, maps, first, count):
    j = iota((8, 384), 0)
    lane = iota((8, 384), 1) - j % 3 * 16
    start = lax.axis_index("tm") * 16 + first
    hot = []
    for f in range(count):
        slot = frame_slot[jnp.minimum(start + f, 127)]
        place = slot // 16 * 48 + slot % 16
        hot.append(jnp.where((lane == place) & (j < 6), 1.0, 0.0))
    hot = jnp.concatenate(hot, axis=0).astype(BF16)
    chosen = jnp.dot(hot, queue[...].reshape(384, 128), preferred_element_type=F32).astype(BF16)
    return jnp.dot(chosen, maps[:, 384:768], preferred_element_type=F32)


def tiles_of(own, rim, lifted):
    tiles = own + rim + [lifted[:, br * 128 : (br + 1) * 128] for br in range(3)]
    return jnp.concatenate(tiles + [jnp.ones((8, 128), F32)], axis=0).astype(BF16)


def stage(inputs, at, frames, maps):
    x = jnp.concatenate(frames, axis=0)
    x = jnp.dot(x, maps[:, 0:384], preferred_element_type=F32).astype(BF16)
    for f in range(len(frames)):
        for dv in range(3):
            inputs[at + f, dv * 80 : (dv + 1) * 80, :] = x[
                f * 80 : (f + 1) * 80, dv * 128 : (dv + 1) * 128
            ]
        inputs[at + f, 240:256, :] = jnp.zeros((16, 128), BF16)


def gains(gain):
    r = lax.axis_index("rows")
    top = jnp.where(r > 0, 0.5, 0.0)
    bottom = jnp.where(r < lax.axis_size("rows") - 1, 0.5, 0.0)
    g = gain[...]
    out = []
    for q in range(5):
        first = g * (top if q == 0 else 0.5)
        second = g * (bottom if q == 4 else 0.5)
        out.append(jnp.concatenate([first, second], axis=1))
    return out


def spread_inputs(inputs, pair):
    return jnp.concatenate([inputs[pair * 2 + b].T for b in range(2)], axis=0)


def norm_act(h, gain, act, q):
    sq = h * h
    parts = []
    for e in range(2):
        lanes = slice(e * 128, (e + 1) * 128)
        ss = jnp.sum(sq[:, lanes], axis=1, keepdims=True)
        scale = lax.rsqrt(ss * (1 / 128) + 1e-6)
        u = h[:, lanes] * scale * gain[:, lanes]
        parts.append(u * jnp.tanh(u) + u)
    s = iota((16, 128), 0)
    for e in range(2):
        a = parts[e].reshape(2, 128, 128)
        act[:, 2 * q + e, 1:9] = a.astype(BF16).reshape(2, 8, 16, 128)
        for b in range(2):
            left = jnp.where(s == 0, 0.0, pltpu.roll(a[b, 112:128], 1, 0))
            right = jnp.where(s == 15, 0.0, pltpu.roll(a[b, 0:16], 15, 0))
            act[b, 2 * q + e, 0] = left.astype(BF16)
            act[b, 2 * q + e, 9] = right.astype(BF16)


def mid_conv(act, w_mid, spatial, at, i):
    frames = []
    for b in range(2):
        taps = [
            act[b, 2 * i + dr, dv : dv + 8].reshape(128, 128) for dr in range(4) for dv in range(3)
        ]
        frames.append(jnp.concatenate(taps, axis=1))
    x = jnp.concatenate(frames, axis=0)
    y = lax.dot_general(w_mid[...], x, NT, preferred_element_type=F32).astype(BF16)
    for b in range(2):
        for e in range(2):
            spatial[i, at + b, :, e * 128 : (e + 1) * 128] = y[
                e * 128 : (e + 1) * 128, b * 128 : (b + 1) * 128
            ]


def network(inputs, pairs, w_in, w_mid, gain, act0, act1, spatial):
    def step(done, pair, todo, following):
        if todo is not None:
            depth = spread_inputs(inputs, following)
            h = jnp.dot(depth, w_in[0], preferred_element_type=F32)
        for q in range(5):
            if done is not None and q < 4:
                mid_conv(done, w_mid, spatial, pair * 2, q)
            if todo is not None:
                now = h
                if q < 4:
                    h = jnp.dot(depth, w_in[q + 1], preferred_element_type=F32)
                norm_act(now, gain[q], todo, q)

    step(None, None, act0, 0)

    @pl.loop(0, pairs // 2 - 1)
    def _(k):
        step(act0, 2 * k, act1, 2 * k + 1)
        step(act1, 2 * k + 1, act0, 2 * k + 2)

    step(act0, pairs - 2, act1, pairs - 1)
    step(act1, pairs - 1, None, None)


def predict(halves, w_mix, w_out, bias_out, total):
    @pl.loop(0, 4)
    def _(i):
        def mixed(g):
            rows = slice(g * 16, (g + 1) * 16)
            x = [ref[i, at : at + 8, rows, :].reshape(128, 256) for ref, at in halves]
            x = jnp.concatenate(x, axis=0)
            return jnp.dot(w_mix[g], x, preferred_element_type=F32) + x.astype(F32)

        acc = None
        following = mixed(0)
        for g in range(8):
            now = following
            if g < 7:
                following = mixed(g + 1)
            h = 0.5 * now
            outer = (h * jnp.tanh(h) + h).astype(BF16)
            p = jnp.dot(w_out[g], outer, preferred_element_type=F32)
            acc = p if acc is None else acc + p
        for o in range(3):
            part = acc[o * 16 : (o + 1) * 16, :] + bias_out[o]
            for e in range(2):
                total[2 * i + e, o * 16 : (o + 1) * 16, :] = part[:, e * 128 : (e + 1) * 128]


def unorder(total, maps, rows):
    x = total[...].reshape(384, 128)
    x0 = x.astype(BF16)
    r = x - x0.astype(F32)
    x1 = r.astype(BF16)
    x2 = (r - x1.astype(F32)).astype(BF16)
    y = [jnp.dot(part, maps[:, 768:896], preferred_element_type=F32) for part in (x0, x1, x2)]
    rows[...] = y[0] + (y[1] + y[2])


def picture(rows, o, f):
    return rows[pl.ds(o * 16 + f, 8, stride=48), :]


def own_kernel(
    frame_slot, own, rim, queue, gain, w_in, w_mid, maps, spatial, inputs, act0, act1
):
    lifted = lift(frame_slot, queue, maps, 0, 16)
    for part in range(4):
        frames = []
        for f in range(part * 4, part * 4 + 4):
            noisy = [own[ch, f].astype(F32) for ch in range(3)]
            edge = [rim[ch, f].astype(F32) for ch in range(3)]
            frames.append(tiles_of(noisy, edge, lifted[f * 8 : f * 8 + 8]))
        stage(inputs, part * 4, frames, maps)
    network(inputs, 8, w_in, w_mid, gains(gain), act0, act1, spatial)


def late_kernel(
    frame_slot, bias_out, ahead, queue, gain, w_in, w_mid, maps, w_mix, w_out, own,
    send, near, inputs, act0, act1, spatial, total, rows,
):
    lifted = lift(frame_slot, queue, maps, 16, 8)
    for part in range(2):
        frames = []
        for f in range(part * 4, part * 4 + 4):
            x = [ahead[ch, f].astype(F32) for ch in range(3)]
            frames.append(
                tiles_of([tile[:8] for tile in x], [tile[8:] for tile in x], lifted[f * 8 : f * 8 + 8])
            )
        stage(inputs, part * 4, frames, maps)
    network(inputs, 4, w_in, w_mid, gains(gain), act0, act1, spatial)
    predict([(own, 8), (spatial, 0)], w_mix, w_out, bias_out, total)
    unorder(total, maps, rows)
    for f in range(8):
        w = ahead[0, f].astype(F32)
        share = w[15:16] / jnp.maximum(w[14:15] + w[15:16], 1.0)
        for o in range(3):
            near[o, f] = picture(rows, o, f)
            send[o, f] = (picture(rows, o, f + 8) * share).astype(BF16)


def early_kernel(bias_out, blend, maps, w_mix, w_out, own, near, mine, total, rows):
    predict([(own, 0), (own, 8)], w_mix, w_out, bias_out, total)
    unorder(total, maps, rows)
    t = lax.axis_index("tm")
    has_prev = jnp.where(t > 0, 1.0, 0.0)
    has_next = jnp.where(t < lax.axis_size("tm") - 1, 1.0, 0.0)
    one = jnp.ones((8, 128), F32)
    for f in range(8):
        lead = one * blend[0, f].astype(F32)
        share = lead / (lead + one * (blend[1, f].astype(F32) * has_prev))
        lead = one * (blend[0, f + 8].astype(F32) * has_next)
        trail = one * blend[1, f + 8].astype(F32)
        for o in range(3):
            mine[o, f] = picture(rows, o, f) * share
            mine[o, f + 8] = (lead * near[o, f] + trail * picture(rows, o, f + 8)) / (lead + trail)


def join_kernel(mine, arrived, out):
    out[:, 0:8] = mine[:, 0:8] + arrived[...].astype(F32)
    out[:, 8:16] = mine[:, 8:16]


def network_scratch(frames):
    act = pltpu.VMEM((2, 10, 10, 16, 128), BF16)
    return [pltpu.VMEM((frames, 256, 128), BF16), act, act]


PICTURES = [pltpu.VMEM((8, 48, 128), F32), pltpu.VMEM((384, 128), F32)]


def shape(dims, kind):
    return jax.ShapeDtypeStruct(dims, kind)


def call(kernel, name, scalars, arrays, outs, scratch_shapes=(), flops=10**8, space=VMEM):
    if space is HBM:
        arrays = [pltpu.with_memory_space_constraint(a, pltpu.HBM) for a in arrays]
    return pl.pallas_call(
        kernel,
        out_shape=outs,
        in_specs=[SMEM] * len(scalars) + [space] * len(arrays),
        out_specs=tuple(VMEM for _ in outs),
        scratch_shapes=list(scratch_shapes),
        compiler_params=PARAMS,
        cost_estimate=pl.CostEstimate(flops=flops, bytes_accessed=10**6, transcendentals=0),
        name=name,
    )(*scalars, *arrays)


def copies_of(arrays):
    return [pltpu.VMEM(a.shape, a.dtype) for a in arrays] + [pltpu.SemaphoreType.DMA((len(arrays),))]


def body(
    noisy_frames, base_queue, frame_slot, blend_weight, weight_in, bias_in, gain_mid, weight_mid,
    time_mix, weight_out, bias_out,
):
    n_t = lax.axis_size("tm")
    n_r = lax.axis_size("rows")
    down = [(i, i + 1) for i in range(n_r - 1)]
    up = [(i + 1, i) for i in range(n_r - 1)]
    back = [(i + 1, i) for i in range(n_t - 1)]
    forth = [(i, i + 1) for i in range(n_t - 1)]
    blend = blend_weight.T
    tile = shape((3, 16, 8, 128), BF16)

    raw = [noisy_frames, jnp.transpose(base_queue[:, :, 0, :], (1, 0, 2))]
    to_below, to_above, base, own = call(
        pack_kernel,
        "pack",
        [],
        raw,
        (tile, tile, shape((48, 128), F32), tile),
        [pltpu.VMEM((384, 128), F32)] + copies_of(raw)[1:],
        space=HBM,
    )
    from_above = lax.ppermute(to_below, "rows", down)
    from_below = lax.ppermute(to_above, "rows", up)
    raw = [
        jnp.asarray(tap_matrix(), BF16),
        weight_in.reshape(9, 6, 128),
        bias_in.reshape(1, 128),
        weight_mid.reshape(9, 128, 128),
        jnp.transpose(time_mix, (1, 2, 0)),
        weight_out.T,
        jnp.asarray(spread_matrix(), BF16),
    ]
    w_in, w_mid, w_mix, w_out, maps = call(
        prepare_kernel,
        "prepare",
        [],
        raw,
        (
            shape((5, 256, 256), BF16),
            shape((256, 1536), BF16),
            shape((8, 256, 256), BF16),
            shape((8, 48, 256), BF16),
            shape((128, 896), BF16),
        ),
        copies_of(raw),
        flops=2 * 10**9,
        space=HBM,
    )
    rim, ask, pack = pl.pallas_call(
        middle_kernel,
        out_shape=(tile, shape((n_t, 48, 128), BF16), shape((3, 8, 16, 128), BF16)),
        in_specs=[HBM] + [VMEM] * 5,
        out_specs=(VMEM,) * 3,
        scratch_shapes=[
            pltpu.VMEM((384, 128), F32),
            pltpu.SMEM((2, 16), jnp.int32),
            pltpu.SemaphoreType.DMA((1,)),
        ],
        compiler_params=PARAMS,
        name="middle",
    )(pltpu.with_memory_space_constraint(blend, pltpu.HBM), own, from_above, from_below, base, maps)
    queue = lax.all_to_all(ask, "tm", 0, 0, tiled=True)
    ahead = lax.ppermute(pack, "tm", back)
    gain = gain_mid.reshape(1, 128)
    (spatial,) = call(
        own_kernel,
        "own",
        [frame_slot],
        [own, rim, queue, gain, w_in, w_mid, maps],
        (shape((4, 16, 128, 256), BF16),),
        network_scratch(16),
        flops=10**10,
    )
    send, near = call(
        late_kernel,
        "late",
        [frame_slot, bias_out],
        [ahead, queue, gain, w_in, w_mid, maps, w_mix, w_out, spatial],
        (shape((3, 8, 8, 128), BF16), shape((3, 8, 8, 128), F32)),
        network_scratch(8) + [pltpu.VMEM((4, 8, 128, 256), BF16)] + PICTURES,
        flops=10**10,
    )
    arrived = lax.ppermute(send, "tm", forth)
    (mine,) = call(
        early_kernel,
        "early",
        [bias_out, blend],
        [maps, w_mix, w_out, spatial, near],
        (shape((3, 16, 8, 128), F32),),
        PICTURES,
        flops=5 * 10**9,
    )
    (out,) = call(join_kernel, "join", [], [mine, arrived], (shape((3, 16, 8, 128), F32),))
    return out


def solution(mesh):
    return jax.shard_map(
        body,
        mesh=mesh,
        in_specs=(
            P(None, "tm", "rows", None),
            P("tm", None, "rows", None),
            P(),
            P("tm", None),
            P(),
            P(),
            P(),
            P(),
            P(),
            P(),
            P(),
        ),
        out_specs=P(None, "tm", "rows", None),
        check_vma=False,
    )
```

```python
import functools

import jax
import jax.numpy as jnp
import numpy as np
from jax import lax
from jax.experimental import pallas as pl
from jax.experimental.pallas import tpu as pltpu
from jax.sharding import PartitionSpec as P

BF16 = jnp.bfloat16
F32 = jnp.float32
NT = (((1,), (1,)), ((), ()))
VMEM = pl.BlockSpec(memory_space=pltpu.VMEM)
HBM = pl.BlockSpec(memory_space=pltpu.HBM)
SMEM = pl.BlockSpec(memory_space=pltpu.SMEM)
PARAMS = pltpu.CompilerParams(vmem_limit_bytes=24 * 2**20)


def tap_matrix():
    m = np.zeros((5, 2, 256, 72), np.float32)
    for q in range(5):
        for e in range(2):
            for dr in range(3):
                row = 2 * q + e - 2 + dr
                for dv in range(3):
                    for ch in range(6):
                        tap = (dr * 3 + dv) * 8 + ch
                        if ch < 3:
                            if 0 <= row < 8:
                                k = ch * 8 + row
                            else:
                                k = 24 + ch * 8 + (row + 2 if row < 0 else row - 6)
                            m[q, e, dv * 80 + k, tap] += 1
                        else:
                            br = 0 if row < 0 else (1 if row < 8 else 2)
                            m[q, e, dv * 80 + 48 + br * 8 + ch - 3, tap] += 1
                            m[q, e, dv * 80 + 48 + br * 8 + ch, tap] += 1
    return m.reshape(10, 256, 72)


def spread_matrix():
    m = np.zeros((496, 256), np.float32)
    m[240 + np.arange(256) // 16, np.arange(256)] = 1
    return m


def iota(shape, dim):
    return lax.broadcasted_iota(jnp.int32, shape, dim)


def fetch(sources, targets, sems):
    copies = [
        pltpu.make_async_copy(source, target, sems.at[i])
        for i, (source, target) in enumerate(zip(sources, targets))
    ]
    for copy in copies:
        copy.start()
    for copy in copies:
        copy.wait()


def pack_kernel(own_hbm, queue_hbm, to_near, to_far, base, own, wide, queue, sems):
    fetch([own_hbm, queue_hbm], [own, queue], sems)
    wide[...] = own[...].astype(F32).reshape(384, 128)
    put = (iota((16, 384), 0) == iota((16, 384), 1) % 128 - iota((16, 384), 1) // 128 * 16).astype(BF16)
    placed = jnp.dot(queue[...].reshape(48, 16), put, preferred_element_type=F32)
    even = lax.rem(lax.axis_index("rows"), 2) == 0
    parts = [
        (wide[pl.ds(6, 48, stride=8), :], wide[pl.ds(0, 48, stride=8), :]),
        (wide[pl.ds(7, 48, stride=8), :], wide[pl.ds(1, 48, stride=8), :]),
        (placed[:, 0:128], placed[:, 256:384]),
    ]
    for k, (down, up) in enumerate(parts):
        to_near[k * 48 : (k + 1) * 48, :] = jnp.where(even, down, up).astype(BF16)
        to_far[k * 48 : (k + 1) * 48, :] = jnp.where(even, up, down).astype(BF16)
    base[...] = placed[:, 128:256].astype(BF16)


def middle_kernel(
    blend_hbm, own, near, far, base, maps, rim, ask, back, both, blend, sems
):
    copy = pltpu.make_async_copy(blend_hbm, blend, sems.at[0])
    copy.start()
    both[...] = jnp.zeros_like(both)
    even = lax.rem(lax.axis_index("rows"), 2) == 0
    for k in range(2):
        x = near[k * 48 : (k + 1) * 48, :].astype(F32)
        y = far[k * 48 : (k + 1) * 48, :].astype(F32)
        both[pl.ds(k, 48, stride=8), :] = jnp.where(even, y, x)
        both[pl.ds(k + 2, 48, stride=8), :] = jnp.where(even, x, y)
    x = both[...].reshape(3, 16, 8, 128)
    rim[...] = x.astype(BF16)
    three = near[96:144, :].astype(F32) + far[96:144, :].astype(F32)
    three = three + base[...].astype(F32)
    three = (three[:24] + pltpu.roll(three[24:], 64, 1)).astype(BF16)
    for i in range(ask.shape[0]):
        ask[i] = three
    copy.wait()
    row = iota((8, 128), 0)
    for ch in range(3):
        for f in range(8):
            y = x[ch, f]
            y = jnp.where(row == 6, blend[0, f].astype(F32), y)
            y = jnp.where(row == 7, blend[1, f].astype(F32), y)
            both_rows = jnp.concatenate([own[ch, f].astype(F32), y], axis=0)
            back[ch, f] = both_rows.astype(BF16)


def prepare_kernel(*refs):
    sources, (w_in, w_mid, w_mix, w_out, maps), targets = refs[:7], refs[7:12], refs[12:19]
    fetch(sources, targets, refs[19])
    taps, win, bias, wmid, mix, wout, over = targets
    col = iota((128, 384), 0)
    lane = iota((128, 384), 1)
    pixel = lane & 127
    maps[:, 0:384] = (col == (pixel & 15) * 8 + (pixel >> 4) + (lane >> 7) - 1).astype(BF16)
    maps[:, 384:768] = (col == (lane >> 7) * 16 + (pixel >> 3)).astype(BF16)
    col = iota((128, 128), 0)
    maps[:, 768:896] = (iota((128, 128), 1) == (col & 15) * 8 + (col >> 4)).astype(BF16)
    k = iota((256, 128), 0)
    low = (k % 80 >= 48) & (k % 80 < 72) & (k % 8 >= 3) & (k % 8 < 6) & (k < 240)
    b = bias[...]
    b0 = b.astype(BF16).astype(F32)
    b1 = (b - b0).astype(BF16).astype(F32)
    b2 = b - b0 - b1
    pad = jnp.zeros((2, 128), F32)
    w = [jnp.concatenate([win[i].astype(F32), pad], axis=0) for i in range(9)]
    w = jnp.concatenate(w, axis=0).astype(BF16)
    for q in range(5):
        for e in range(2):
            v = jnp.dot(taps[2 * q + e], w, preferred_element_type=F32)
            v = jnp.where(low, v - v.astype(BF16).astype(F32), v)
            v = jnp.where(k == 152, b0, jnp.where(k == 153, b1, jnp.where(k == 154, b2, v)))
            w_in[q, :, e * 128 : (e + 1) * 128] = v.astype(BF16)
    none = jnp.zeros((128, 384), BF16)
    w_mid[0:128, 1152:1536] = none
    w_mid[128:256, 0:384] = none
    for dr in range(3):
        for dv in range(3):
            t = wmid[dr * 3 + dv].T
            for e in range(2):
                tap = (dr + e) * 3 + dv
                w_mid[e * 128 : (e + 1) * 128, tap * 128 : (tap + 1) * 128] = t
    flat = mix[...].reshape(256, 128)
    flat = jnp.concatenate([flat[:128].T, flat[128:].T], axis=1)
    same = iota((128, 256), 0) % 16 == iota((128, 256), 1) % 16
    for p in range(16):
        t = jnp.dot(flat, over[240 - 16 * p : 496 - 16 * p, :], preferred_element_type=F32)
        t = jnp.where(same, t, 0.0).astype(BF16)
        for g in range(8):
            w_mix[g, p * 16 : (p + 1) * 16, :] = t[g * 16 : (g + 1) * 16, :]
    own = iota((16, 256), 0) == iota((16, 256), 1) // 16
    wo = jnp.concatenate([wout[...].astype(F32), jnp.zeros((5, 128), F32)], axis=0).astype(BF16)
    for g in range(8):
        pick = (iota((128, 256), 0) == g * 16 + iota((128, 256), 1) % 16).astype(BF16)
        t = jnp.dot(wo, pick, preferred_element_type=F32)
        for o in range(3):
            w_out[g, o * 16 : (o + 1) * 16, :] = jnp.where(own, t[o : o + 1, :], 0.0).astype(BF16)


def lift(frame_slot, queue, maps, first, count):
    j = iota((8, 384), 0)
    lane = iota((8, 384), 1)
    start = lax.axis_index("tm") * 16 + first
    hot = []
    for f in range(count):
        slot = frame_slot[jnp.minimum(start + f, 127)]
        row = j % 3 * 16 + slot % 16
        place = slot // 16 * 24 + jnp.where(row < 24, row, row + 168)
        hot.append(jnp.where((lane == place) & (j < 6), 1.0, 0.0))
    hot = jnp.concatenate(hot, axis=0).astype(BF16)
    rows = queue[...].astype(F32).reshape(192, 128)
    rows = jnp.concatenate([rows, pltpu.roll(rows, 64, 1)], axis=0).astype(BF16)
    chosen = jnp.dot(hot, rows, preferred_element_type=F32).astype(BF16)
    return jnp.dot(chosen, maps[:, 384:768], preferred_element_type=F32)


def tiles_of(own, rim, lifted):
    tiles = own + rim + [lifted[:, br * 128 : (br + 1) * 128] for br in range(3)]
    return jnp.concatenate(tiles + [jnp.ones((8, 128), F32)], axis=0).astype(BF16)


def stage(inputs, at, frames, maps):
    x = jnp.concatenate(frames, axis=0)
    x = jnp.dot(x, maps[:, 0:384], preferred_element_type=F32).astype(BF16)
    for f in range(len(frames)):
        for dv in range(3):
            inputs[at + f, dv * 80 : (dv + 1) * 80, :] = x[
                f * 80 : (f + 1) * 80, dv * 128 : (dv + 1) * 128
            ]
        inputs[at + f, 240:256, :] = jnp.zeros((16, 128), BF16)


def gains(gain):
    r = lax.axis_index("rows")
    top = jnp.where(r > 0, 0.5, 0.0)
    bottom = jnp.where(r < lax.axis_size("rows") - 1, 0.5, 0.0)
    g = gain[...]
    out = []
    for q in range(5):
        first = g * (top if q == 0 else 0.5)
        second = g * (bottom if q == 4 else 0.5)
        out.append(jnp.concatenate([first, second], axis=1))
    return out


def spread_inputs(inputs, pair):
    return jnp.concatenate([inputs[pair * 2 + b].T for b in range(2)], axis=0)


def norm_act(h, gain, act, q):
    sq = h * h
    parts = []
    for e in range(2):
        lanes = slice(e * 128, (e + 1) * 128)
        ss = jnp.sum(sq[:, lanes], axis=1, keepdims=True)
        scale = lax.rsqrt(ss * (1 / 128) + 1e-6)
        u = h[:, lanes] * scale * gain[:, lanes]
        parts.append(u * jnp.tanh(u) + u)
    s = iota((16, 128), 0)
    for e in range(2):
        a = parts[e].reshape(2, 128, 128)
        act[:, 2 * q + e, 1:9] = a.astype(BF16).reshape(2, 8, 16, 128)
        for b in range(2):
            left = jnp.where(s == 0, 0.0, pltpu.roll(a[b, 112:128], 1, 0))
            right = jnp.where(s == 15, 0.0, pltpu.roll(a[b, 0:16], 15, 0))
            act[b, 2 * q + e, 0] = left.astype(BF16)
            act[b, 2 * q + e, 9] = right.astype(BF16)


def mid_conv(act, w_mid, spatial, at, i):
    frames = []
    for b in range(2):
        taps = [
            act[b, 2 * i + dr, dv : dv + 8].reshape(128, 128) for dr in range(4) for dv in range(3)
        ]
        frames.append(jnp.concatenate(taps, axis=1))
    x = jnp.concatenate(frames, axis=0)
    y = lax.dot_general(w_mid[...], x, NT, preferred_element_type=F32).astype(BF16)
    for b in range(2):
        for e in range(2):
            spatial[i, at + b, :, e * 128 : (e + 1) * 128] = y[
                e * 128 : (e + 1) * 128, b * 128 : (b + 1) * 128
            ]


def network(inputs, pairs, w_in, w_mid, gain, act0, act1, spatial):
    def step(done, pair, todo, following):
        if todo is not None:
            depth = spread_inputs(inputs, following)
            h = jnp.dot(depth, w_in[0], preferred_element_type=F32)
        for q in range(5):
            if done is not None and q < 4:
                mid_conv(done, w_mid, spatial, pair * 2, q)
            if todo is not None:
                now = h
                if q < 4:
                    h = jnp.dot(depth, w_in[q + 1], preferred_element_type=F32)
                norm_act(now, gain[q], todo, q)

    acts = [act0, act1]
    step(None, None, act0, 0)
    for p in range(pairs):
        step(acts[p % 2], p, acts[1 - p % 2] if p < pairs - 1 else None, p + 1)


def predict(halves, w_mix, w_out, bias_out, total):
    def mixed(i, g):
        rows = slice(g * 16, (g + 1) * 16)
        x = [ref[i, at : at + 8, rows, :].reshape(128, 256) for ref, at in halves]
        x = jnp.concatenate(x, axis=0)
        return jnp.dot(w_mix[g], x, preferred_element_type=F32) + x.astype(F32)

    @pl.loop(0, 2)
    def _(k):
        order = [(2 * k + u, g) for u in range(2) for g in range(8)]
        following = mixed(*order[0])
        for n, (i, g) in enumerate(order):
            now = following
            if n < 15:
                following = mixed(*order[n + 1])
            h = 0.5 * now
            outer = (h * jnp.tanh(h) + h).astype(BF16)
            if g % 2 == 0:
                held = outer
                continue
            w = jnp.concatenate([w_out[g - 1], w_out[g]], axis=1)
            p = jnp.dot(w, jnp.concatenate([held, outer], axis=0), preferred_element_type=F32)
            acc = p if g == 1 else acc + p
            if g == 7:
                for o in range(3):
                    part = acc[o * 16 : (o + 1) * 16, :] + bias_out[o]
                    for e in range(2):
                        total[2 * i + e, o * 16 : (o + 1) * 16, :] = part[:, e * 128 : (e + 1) * 128]


def unorder(total, maps, rows):
    x = total[...].reshape(384, 128)
    x0 = x.astype(BF16)
    r = x - x0.astype(F32)
    x1 = r.astype(BF16)
    x2 = (r - x1.astype(F32)).astype(BF16)
    y = [jnp.dot(part, maps[:, 768:896], preferred_element_type=F32) for part in (x0, x1, x2)]
    rows[...] = y[0] + (y[1] + y[2])


def picture(rows, o, f):
    return rows[pl.ds(o * 16 + f, 8, stride=48), :]


def own_kernel(
    frame_slot, own, rim, queue, gain, w_in, w_mid, maps, spatial, inputs, act0, act1
):
    lifted = lift(frame_slot, queue, maps, 0, 16)
    for part in range(4):
        frames = []
        for f in range(part * 4, part * 4 + 4):
            noisy = [own[ch, f].astype(F32) for ch in range(3)]
            edge = [rim[ch, f].astype(F32) for ch in range(3)]
            frames.append(tiles_of(noisy, edge, lifted[f * 8 : f * 8 + 8]))
        stage(inputs, part * 4, frames, maps)
    network(inputs, 8, w_in, w_mid, gains(gain), act0, act1, spatial)


def late_kernel(
    frame_slot, bias_out, ahead, queue, gain, w_in, w_mid, maps, w_mix, w_out, own,
    send, near, inputs, act0, act1, spatial, total, rows,
):
    lifted = lift(frame_slot, queue, maps, 16, 8)
    for part in range(2):
        frames = []
        for f in range(part * 4, part * 4 + 4):
            x = [ahead[ch, f].astype(F32) for ch in range(3)]
            frames.append(
                tiles_of([tile[:8] for tile in x], [tile[8:] for tile in x], lifted[f * 8 : f * 8 + 8])
            )
        stage(inputs, part * 4, frames, maps)
    network(inputs, 4, w_in, w_mid, gains(gain), act0, act1, spatial)
    predict([(own, 8), (spatial, 0)], w_mix, w_out, bias_out, total)
    unorder(total, maps, rows)
    for f in range(8):
        w = ahead[0, f].astype(F32)
        share = w[15:16] / jnp.maximum(w[14:15] + w[15:16], 1.0)
        for o in range(3):
            near[o, f] = picture(rows, o, f)
            send[o, f] = (picture(rows, o, f + 8) * share).astype(BF16)


def early_kernel(bias_out, blend, maps, w_mix, w_out, own, near, mine, total, rows):
    predict([(own, 0), (own, 8)], w_mix, w_out, bias_out, total)
    unorder(total, maps, rows)
    t = lax.axis_index("tm")
    has_prev = jnp.where(t > 0, 1.0, 0.0)
    has_next = jnp.where(t < lax.axis_size("tm") - 1, 1.0, 0.0)
    one = jnp.ones((8, 128), F32)
    for f in range(8):
        lead = one * blend[0, f].astype(F32)
        share = lead / (lead + one * (blend[1, f].astype(F32) * has_prev))
        lead = one * (blend[0, f + 8].astype(F32) * has_next)
        trail = one * blend[1, f + 8].astype(F32)
        for o in range(3):
            mine[o, f] = picture(rows, o, f) * share
            mine[o, f + 8] = (lead * near[o, f] + trail * picture(rows, o, f + 8)) / (lead + trail)


def join_kernel(mine, arrived, out):
    out[:, 0:8] = mine[:, 0:8] + arrived[...].astype(F32)
    out[:, 8:16] = mine[:, 8:16]


def network_scratch(frames):
    act = pltpu.VMEM((2, 10, 10, 16, 128), BF16)
    return [pltpu.VMEM((frames, 256, 128), BF16), act, act]


PICTURES = [pltpu.VMEM((8, 48, 128), F32), pltpu.VMEM((384, 128), F32)]


def shape(dims, kind):
    return jax.ShapeDtypeStruct(dims, kind)


def call(kernel, name, scalars, arrays, outs, scratch_shapes=(), flops=10**8, space=VMEM):
    if space is HBM:
        arrays = [pltpu.with_memory_space_constraint(a, pltpu.HBM) for a in arrays]
    return pl.pallas_call(
        kernel,
        out_shape=outs,
        in_specs=[SMEM] * len(scalars) + [space] * len(arrays),
        out_specs=tuple(VMEM for _ in outs),
        scratch_shapes=list(scratch_shapes),
        compiler_params=PARAMS,
        cost_estimate=pl.CostEstimate(flops=flops, bytes_accessed=10**6, transcendentals=0),
        name=name,
    )(*scalars, *arrays)


def copies_of(arrays):
    return [pltpu.VMEM(a.shape, a.dtype) for a in arrays] + [pltpu.SemaphoreType.DMA((len(arrays),))]


def body(
    noisy_frames, base_queue, frame_slot, blend_weight, weight_in, bias_in, gain_mid, weight_mid,
    time_mix, weight_out, bias_out,
):
    n_t = lax.axis_size("tm")
    n_r = lax.axis_size("rows")
    near = [(i, i ^ 1) for i in range(n_r)]
    far = [(i, (i - 1 ^ 1) + 1) for i in range(1, n_r - 1)]
    back = [(i + 1, i) for i in range(n_t - 1)]
    forth = [(i, i + 1) for i in range(n_t - 1)]
    blend = blend_weight.T
    tile = shape((3, 16, 8, 128), BF16)

    raw = [noisy_frames, jnp.transpose(base_queue[:, :, 0, :], (1, 0, 2))]
    to_near, to_far, base, own = call(
        pack_kernel,
        "pack",
        [],
        raw,
        (shape((144, 128), BF16), shape((144, 128), BF16), shape((48, 128), BF16), tile),
        [pltpu.VMEM((384, 128), F32)] + copies_of(raw)[1:],
        space=HBM,
    )
    from_far = lax.ppermute(to_far, "rows", far)
    from_near = lax.ppermute(to_near, "rows", near)
    raw = [
        jnp.asarray(tap_matrix(), BF16),
        weight_in.reshape(9, 6, 128),
        bias_in.reshape(1, 128),
        weight_mid.reshape(9, 128, 128),
        jnp.transpose(time_mix, (1, 2, 0)),
        weight_out.T,
        jnp.asarray(spread_matrix(), BF16),
    ]
    w_in, w_mid, w_mix, w_out, maps = call(
        prepare_kernel,
        "prepare",
        [],
        raw,
        (
            shape((5, 256, 256), BF16),
            shape((256, 1536), BF16),
            shape((8, 256, 256), BF16),
            shape((8, 48, 256), BF16),
            shape((128, 896), BF16),
        ),
        copies_of(raw),
        flops=2 * 10**9,
        space=HBM,
    )
    rim, ask, pack = pl.pallas_call(
        middle_kernel,
        out_shape=(tile, shape((n_t, 24, 128), BF16), shape((3, 8, 16, 128), BF16)),
        in_specs=[HBM] + [VMEM] * 5,
        out_specs=(VMEM,) * 3,
        scratch_shapes=[
            pltpu.VMEM((384, 128), F32),
            pltpu.SMEM((2, 16), jnp.int32),
            pltpu.SemaphoreType.DMA((1,)),
        ],
        compiler_params=PARAMS,
        name="middle",
    )(pltpu.with_memory_space_constraint(blend, pltpu.HBM), own, from_near, from_far, base, maps)
    queue = lax.all_to_all(ask, "tm", 0, 0, tiled=True)
    ahead = lax.ppermute(pack, "tm", back)
    gain = gain_mid.reshape(1, 128)
    (spatial,) = call(
        own_kernel,
        "own",
        [frame_slot],
        [own, rim, queue, gain, w_in, w_mid, maps],
        (shape((4, 16, 128, 256), BF16),),
        network_scratch(16),
        flops=10**10,
    )
    send, next_half = call(
        late_kernel,
        "late",
        [frame_slot, bias_out],
        [ahead, queue, gain, w_in, w_mid, maps, w_mix, w_out, spatial],
        (shape((3, 8, 8, 128), BF16), shape((3, 8, 8, 128), F32)),
        network_scratch(8) + [pltpu.VMEM((4, 8, 128, 256), BF16)] + PICTURES,
        flops=10**10,
    )
    arrived = lax.ppermute(send, "tm", forth)
    (mine,) = call(
        early_kernel,
        "early",
        [bias_out, blend],
        [maps, w_mix, w_out, spatial, next_half],
        (shape((3, 16, 8, 128), F32),),
        PICTURES,
        flops=5 * 10**9,
    )
    (out,) = call(join_kernel, "join", [], [mine, arrived], (shape((3, 16, 8, 128), F32),))
    return out


def solution(mesh):
    return jax.shard_map(
        body,
        mesh=mesh,
        in_specs=(
            P(None, "tm", "rows", None),
            P("tm", None, "rows", None),
            P(),
            P("tm", None),
            P(),
            P(),
            P(),
            P(),
            P(),
            P(),
            P(),
        ),
        out_specs=P(None, "tm", "rows", None),
        check_vma=False,
    )
```

```python
import functools

import jax
import jax.numpy as jnp
import numpy as np
from jax import lax
from jax.experimental import pallas as pl
from jax.experimental.pallas import tpu as pltpu
from jax.sharding import PartitionSpec as P

BF16 = jnp.bfloat16
F32 = jnp.float32
NT = (((1,), (1,)), ((), ()))
VMEM = pl.BlockSpec(memory_space=pltpu.VMEM)
HBM = pl.BlockSpec(memory_space=pltpu.HBM)
SMEM = pl.BlockSpec(memory_space=pltpu.SMEM)
PARAMS = pltpu.CompilerParams(vmem_limit_bytes=24 * 2**20)


def tap_matrix():
    m = np.zeros((5, 2, 256, 72), np.float32)
    for q in range(5):
        for e in range(2):
            for dr in range(3):
                row = 2 * q + e - 2 + dr
                for dv in range(3):
                    for ch in range(6):
                        tap = (dr * 3 + dv) * 8 + ch
                        if ch < 3:
                            if 0 <= row < 8:
                                k = ch * 8 + row
                            else:
                                k = 24 + ch * 8 + (row + 2 if row < 0 else row - 6)
                            m[q, e, dv * 80 + k, tap] += 1
                        else:
                            br = 0 if row < 0 else (1 if row < 8 else 2)
                            m[q, e, dv * 80 + 48 + br * 8 + ch - 3, tap] += 1
                            m[q, e, dv * 80 + 48 + br * 8 + ch, tap] += 1
    return m.reshape(10, 256, 72)


def spread_matrix():
    m = np.zeros((496, 256), np.float32)
    m[240 + np.arange(256) // 16, np.arange(256)] = 1
    return m


def iota(shape, dim):
    return lax.broadcasted_iota(jnp.int32, shape, dim)


def fetch(sources, targets, sems):
    copies = [
        pltpu.make_async_copy(source, target, sems.at[i])
        for i, (source, target) in enumerate(zip(sources, targets))
    ]
    for copy in copies:
        copy.start()
    for copy in copies:
        copy.wait()


def pack_kernel(own_hbm, queue_hbm, to_near, to_far, base, own, wide, queue, sems):
    fetch([own_hbm, queue_hbm], [own, queue], sems)
    wide[...] = own[...].astype(F32).reshape(384, 128)
    put = (iota((16, 384), 0) == iota((16, 384), 1) % 128 - iota((16, 384), 1) // 128 * 16).astype(BF16)
    placed = jnp.dot(queue[...].reshape(48, 16), put, preferred_element_type=F32)
    even = lax.rem(lax.axis_index("rows"), 2) == 0
    parts = [
        (wide[pl.ds(6, 48, stride=8), :], wide[pl.ds(0, 48, stride=8), :]),
        (wide[pl.ds(7, 48, stride=8), :], wide[pl.ds(1, 48, stride=8), :]),
        (placed[:, 0:128], placed[:, 256:384]),
    ]
    for k, (down, up) in enumerate(parts):
        to_near[k * 48 : (k + 1) * 48, :] = jnp.where(even, down, up).astype(BF16)
        to_far[k * 48 : (k + 1) * 48, :] = jnp.where(even, up, down).astype(BF16)
    base[...] = placed[:, 128:256].astype(BF16)


def middle_kernel(own, near, far, base, weights, rim, ask, back, both):
    both[...] = jnp.zeros_like(both)
    even = lax.rem(lax.axis_index("rows"), 2) == 0
    for k in range(2):
        x = near[k * 48 : (k + 1) * 48, :].astype(F32)
        y = far[k * 48 : (k + 1) * 48, :].astype(F32)
        both[pl.ds(k, 48, stride=8), :] = jnp.where(even, y, x)
        both[pl.ds(k + 2, 48, stride=8), :] = jnp.where(even, x, y)
    x = both[...].reshape(3, 16, 8, 128)
    rim[...] = x.astype(BF16)
    three = near[96:144, :].astype(F32) + far[96:144, :].astype(F32)
    three = three + base[...].astype(F32)
    three = (three[:24] + pltpu.roll(three[24:], 64, 1)).astype(BF16)
    for i in range(ask.shape[0]):
        ask[i] = three
    row = iota((8, 128), 0)
    for ch in range(3):
        for f in range(8):
            y = jnp.where(row == 6, weights[f : f + 1, :], x[ch, f])
            y = jnp.where(row == 7, weights[f + 8 : f + 9, :], y)
            both_rows = jnp.concatenate([own[ch, f].astype(F32), y], axis=0)
            back[ch, f] = both_rows.astype(BF16)


def selection(frame_slot):
    j = iota((8, 384), 0)
    lane = iota((8, 384), 1)
    start = lax.axis_index("tm") * 16
    hot = []
    for f in range(24):
        slot = frame_slot[jnp.minimum(start + f, 127)]
        row = j % 3 * 16 + slot % 16
        place = slot // 16 * 24 + jnp.where(row < 24, row, row + 168)
        hot.append(jnp.where((lane == place) & (j < 6), 1.0, 0.0))
    return jnp.concatenate(hot, axis=0).astype(BF16)


def blend_shares(blend):
    t = lax.axis_index("tm")
    has_prev = jnp.where(t > 0, 1.0, 0.0)
    has_next = jnp.where(t < lax.axis_size("tm") - 1, 1.0, 0.0)
    row = iota((16, 128), 0)
    lead = jnp.zeros((16, 128), F32)
    trail = jnp.zeros((16, 128), F32)
    for f in range(16):
        lead = jnp.where(row == f, blend[0, f].astype(F32), lead)
        trail = jnp.where(row == f, blend[1, f].astype(F32), trail)
    raw = jnp.concatenate([lead[0:8], trail[0:8]], axis=0)
    lead = jnp.where(row < 8, lead, lead * has_next)
    trail = jnp.where(row < 8, trail * has_prev, trail)
    total = lead + trail
    return raw, jnp.concatenate([lead / total, trail / total], axis=0)


def prepare_kernel(*refs):
    sources, made, targets, sems = refs[:10], refs[10:19], refs[19:29], refs[29]
    fetch(sources, targets, sems)
    taps, win, bias, wmid, mix, wout, over, blend, frame_slot, bias_out = targets
    w_in, w_mid, w_mix, w_out, maps, weights, shares, hot, offset = made
    weights[...], shares[...] = blend_shares(blend)
    hot[...] = selection(frame_slot)
    for o in range(3):
        offset[o * 16 : (o + 1) * 16, :] = jnp.zeros((16, 128), F32) + bias_out[o]
    col = iota((128, 384), 0)
    lane = iota((128, 384), 1)
    pixel = lane & 127
    maps[:, 0:384] = (col == (pixel & 15) * 8 + (pixel >> 4) + (lane >> 7) - 1).astype(BF16)
    maps[:, 384:768] = (col == (lane >> 7) * 16 + (pixel >> 3)).astype(BF16)
    col = iota((128, 128), 0)
    maps[:, 768:896] = (iota((128, 128), 1) == (col & 15) * 8 + (col >> 4)).astype(BF16)
    k = iota((256, 128), 0)
    low = (k % 80 >= 48) & (k % 80 < 72) & (k % 8 >= 3) & (k % 8 < 6) & (k < 240)
    b = bias[...]
    b0 = b.astype(BF16).astype(F32)
    b1 = (b - b0).astype(BF16).astype(F32)
    b2 = b - b0 - b1
    pad = jnp.zeros((2, 128), F32)
    w = [jnp.concatenate([win[i].astype(F32), pad], axis=0) for i in range(9)]
    w = jnp.concatenate(w, axis=0).astype(BF16)
    for q in range(5):
        for e in range(2):
            v = jnp.dot(taps[2 * q + e], w, preferred_element_type=F32)
            v = jnp.where(low, v - v.astype(BF16).astype(F32), v)
            v = jnp.where(k == 152, b0, jnp.where(k == 153, b1, jnp.where(k == 154, b2, v)))
            w_in[q, :, e * 128 : (e + 1) * 128] = v.astype(BF16)
    none = jnp.zeros((128, 384), BF16)
    w_mid[0:128, 1152:1536] = none
    w_mid[128:256, 0:384] = none
    for dr in range(3):
        for dv in range(3):
            t = wmid[dr * 3 + dv].T
            for e in range(2):
                tap = (dr + e) * 3 + dv
                w_mid[e * 128 : (e + 1) * 128, tap * 128 : (tap + 1) * 128] = t
    flat = mix[...].reshape(256, 128)
    flat = jnp.concatenate([flat[:128].T, flat[128:].T], axis=1)
    same = iota((128, 256), 0) % 16 == iota((128, 256), 1) % 16
    for p in range(16):
        t = jnp.dot(flat, over[240 - 16 * p : 496 - 16 * p, :], preferred_element_type=F32)
        t = jnp.where(same, t, 0.0).astype(BF16)
        for g in range(8):
            w_mix[g, p * 16 : (p + 1) * 16, :] = t[g * 16 : (g + 1) * 16, :]
    own = iota((16, 256), 0) == iota((16, 256), 1) // 16
    wo = jnp.concatenate([wout[...].astype(F32), jnp.zeros((5, 128), F32)], axis=0).astype(BF16)
    for g in range(8):
        pick = (iota((128, 256), 0) == g * 16 + iota((128, 256), 1) % 16).astype(BF16)
        t = jnp.dot(wo, pick, preferred_element_type=F32)
        for o in range(3):
            w_out[g, o * 16 : (o + 1) * 16, :] = jnp.where(own, t[o : o + 1, :], 0.0).astype(BF16)


def lift(hot, queue, maps):
    rows = queue[...].astype(F32).reshape(192, 128)
    rows = jnp.concatenate([rows, pltpu.roll(rows, 64, 1)], axis=0).astype(BF16)
    chosen = jnp.dot(hot[...], rows, preferred_element_type=F32).astype(BF16)
    return jnp.dot(chosen, maps[:, 384:768], preferred_element_type=F32)


def tiles_of(own, rim, lifted):
    tiles = own + rim + [lifted[:, br * 128 : (br + 1) * 128] for br in range(3)]
    return jnp.concatenate(tiles + [jnp.ones((8, 128), F32)], axis=0).astype(BF16)


def stage(inputs, at, frames, maps):
    x = jnp.concatenate(frames, axis=0)
    x = jnp.dot(x, maps[:, 0:384], preferred_element_type=F32).astype(BF16)
    for f in range(len(frames)):
        for dv in range(3):
            inputs[at + f, dv * 80 : (dv + 1) * 80, :] = x[
                f * 80 : (f + 1) * 80, dv * 128 : (dv + 1) * 128
            ]
        inputs[at + f, 240:256, :] = jnp.zeros((16, 128), BF16)


def gains(gain):
    r = lax.axis_index("rows")
    top = jnp.where(r > 0, 0.5, 0.0)
    bottom = jnp.where(r < lax.axis_size("rows") - 1, 0.5, 0.0)
    g = gain[...]
    out = []
    for q in range(5):
        first = g * (top if q == 0 else 0.5)
        second = g * (bottom if q == 4 else 0.5)
        out.append(jnp.concatenate([first, second], axis=1))
    return out


def spread_inputs(inputs, pair):
    return jnp.concatenate([inputs[pair * 2 + b].T for b in range(2)], axis=0)


def norm_act(h, gain, act, q):
    sq = h * h
    parts = []
    for e in range(2):
        lanes = slice(e * 128, (e + 1) * 128)
        ss = jnp.sum(sq[:, lanes], axis=1, keepdims=True)
        scale = lax.rsqrt(ss * (1 / 128) + 1e-6)
        u = h[:, lanes] * scale * gain[:, lanes]
        parts.append(u * jnp.tanh(u) + u)
    s = iota((16, 128), 0)
    for e in range(2):
        a = parts[e].reshape(2, 128, 128)
        act[:, 2 * q + e, 1:9] = a.astype(BF16).reshape(2, 8, 16, 128)
        for b in range(2):
            left = jnp.where(s == 0, 0.0, pltpu.roll(a[b, 112:128], 1, 0))
            right = jnp.where(s == 15, 0.0, pltpu.roll(a[b, 0:16], 15, 0))
            act[b, 2 * q + e, 0] = left.astype(BF16)
            act[b, 2 * q + e, 9] = right.astype(BF16)


def mid_conv(act, w_mid, spatial, at, i):
    frames = []
    for b in range(2):
        taps = [
            act[b, 2 * i + dr, dv : dv + 8].reshape(128, 128) for dr in range(4) for dv in range(3)
        ]
        frames.append(jnp.concatenate(taps, axis=1))
    x = jnp.concatenate(frames, axis=0)
    y = lax.dot_general(w_mid[...], x, NT, preferred_element_type=F32).astype(BF16)
    for b in range(2):
        for e in range(2):
            spatial[i, at + b, :, e * 128 : (e + 1) * 128] = y[
                e * 128 : (e + 1) * 128, b * 128 : (b + 1) * 128
            ]


def network(inputs, pairs, frame, maps, w_in, w_mid, gain, act0, act1, spatial):
    def step(done, pair, todo, following):
        if todo is not None:
            depth = spread_inputs(inputs, following)
            h = jnp.dot(depth, w_in[0], preferred_element_type=F32)
        for q in range(5):
            if done is not None and q < 4:
                mid_conv(done, w_mid, spatial, pair * 2, q)
            if todo is not None:
                now = h
                if q < 4:
                    h = jnp.dot(depth, w_in[q + 1], preferred_element_type=F32)
                norm_act(now, gain[q], todo, q)

    for part in range(pairs // 2):
        stage(inputs, part * 4, [frame(part * 4 + f) for f in range(4)], maps)
    acts = [act0, act1]
    step(None, None, act0, 0)
    for p in range(pairs):
        step(acts[p % 2], p, acts[1 - p % 2] if p < pairs - 1 else None, p + 1)


def predict(halves, w_mix, w_out, offset, total):
    def mixed(i, g):
        rows = slice(g * 16, (g + 1) * 16)
        x = [ref[i, at : at + 8, rows, :].reshape(128, 256) for ref, at in halves]
        x = jnp.concatenate(x, axis=0)
        return jnp.dot(w_mix[g], x, preferred_element_type=F32) + x.astype(F32)

    order = [(i, g) for i in range(4) for g in range(8)]
    queued = [mixed(*order[n]) for n in range(3)]
    for n, (i, g) in enumerate(order):
        now = queued.pop(0)
        if n + 3 < len(order):
            queued.append(mixed(*order[n + 3]))
        h = 0.5 * now
        outer = (h * jnp.tanh(h) + h).astype(BF16)
        if g % 2 == 0:
            held = outer
            continue
        w = jnp.concatenate([w_out[g - 1], w_out[g]], axis=1)
        p = jnp.dot(w, jnp.concatenate([held, outer], axis=0), preferred_element_type=F32)
        acc = p if g == 1 else acc + p
        if g == 7:
            for e in range(2):
                total[2 * i + e] = acc[:, e * 128 : (e + 1) * 128] + offset[...]


def unorder(total, maps, rows):
    x = total[...].reshape(384, 128)
    x0 = x.astype(BF16)
    r = x - x0.astype(F32)
    x1 = r.astype(BF16)
    x2 = (r - x1.astype(F32)).astype(BF16)
    y = [jnp.dot(part, maps[:, 768:896], preferred_element_type=F32) for part in (x0, x1, x2)]
    rows[...] = y[0] + (y[1] + y[2])


def picture(rows, o, f):
    return rows[pl.ds(o * 16 + f, 8, stride=48), :]


def own_kernel(
    hot, own, rim, queue, gain, w_in, w_mid, maps, spatial, lifted_ahead, inputs, act0, act1
):
    lifted = lift(hot, queue, maps)
    lifted_ahead[...] = lifted[128:]

    def frame(f):
        noisy = [own[ch, f].astype(F32) for ch in range(3)]
        edge = [rim[ch, f].astype(F32) for ch in range(3)]
        return tiles_of(noisy, edge, lifted[f * 8 : f * 8 + 8])

    network(inputs, 8, frame, maps, w_in, w_mid, gains(gain), act0, act1, spatial)


def late_kernel(
    offset, ahead, lifted, gain, w_in, w_mid, maps, w_mix, w_out, own,
    send, near, inputs, act0, act1, spatial, total, rows,
):
    def frame(f):
        x = [ahead[ch, f].astype(F32) for ch in range(3)]
        noisy, edge = [tile[:8] for tile in x], [tile[8:] for tile in x]
        return tiles_of(noisy, edge, lifted[f * 8 : f * 8 + 8, :])

    network(inputs, 4, frame, maps, w_in, w_mid, gains(gain), act0, act1, spatial)
    predict([(own, 8), (spatial, 0)], w_mix, w_out, offset, total)
    unorder(total, maps, rows)
    for f in range(8):
        w = ahead[0, f].astype(F32)
        share = w[15:16] / jnp.maximum(w[14:15] + w[15:16], 1.0)
        for o in range(3):
            near[o, f] = picture(rows, o, f)
            send[o, f] = (picture(rows, o, f + 8) * share).astype(BF16)


def early_kernel(offset, shares, maps, w_mix, w_out, own, near, mine, total, rows):
    predict([(own, 0), (own, 8)], w_mix, w_out, offset, total)
    unorder(total, maps, rows)
    for f in range(16):
        lead, trail = shares[f : f + 1, :], shares[f + 16 : f + 17, :]
        for o in range(3):
            if f < 8:
                mine[o, f] = picture(rows, o, f) * lead
            else:
                mine[o, f] = near[o, f - 8] * lead + picture(rows, o, f) * trail


def join_kernel(mine, arrived, out):
    out[:, 0:8] = mine[:, 0:8] + arrived[...].astype(F32)
    out[:, 8:16] = mine[:, 8:16]


def network_scratch(frames):
    act = pltpu.VMEM((2, 10, 10, 16, 128), BF16)
    return [pltpu.VMEM((frames, 256, 128), BF16), act, act]


PICTURES = [pltpu.VMEM((8, 48, 128), F32), pltpu.VMEM((384, 128), F32)]


def shape(dims, kind):
    return jax.ShapeDtypeStruct(dims, kind)


def call(kernel, name, scalars, arrays, outs, scratch_shapes=(), flops=10**8, space=VMEM):
    if space is HBM:
        arrays = [pltpu.with_memory_space_constraint(a, pltpu.HBM) for a in arrays]
    return pl.pallas_call(
        kernel,
        out_shape=outs,
        in_specs=[SMEM] * len(scalars) + [space] * len(arrays),
        out_specs=tuple(VMEM for _ in outs),
        scratch_shapes=list(scratch_shapes),
        compiler_params=PARAMS,
        cost_estimate=pl.CostEstimate(flops=flops, bytes_accessed=10**6, transcendentals=0),
        name=name,
    )(*scalars, *arrays)


def copies_of(arrays):
    return [pltpu.VMEM(a.shape, a.dtype) for a in arrays] + [pltpu.SemaphoreType.DMA((len(arrays),))]


def body(
    noisy_frames, base_queue, frame_slot, blend_weight, weight_in, bias_in, gain_mid, weight_mid,
    time_mix, weight_out, bias_out,
):
    n_t = lax.axis_size("tm")
    n_r = lax.axis_size("rows")
    near = [(i, i ^ 1) for i in range(n_r)]
    far = [(i, (i - 1 ^ 1) + 1) for i in range(1, n_r - 1)]
    back = [(i + 1, i) for i in range(n_t - 1)]
    forth = [(i, i + 1) for i in range(n_t - 1)]
    blend = blend_weight.T
    tile = shape((3, 16, 8, 128), BF16)

    raw = [noisy_frames, jnp.transpose(base_queue[:, :, 0, :], (1, 0, 2))]
    to_near, to_far, base, own = call(
        pack_kernel,
        "pack",
        [],
        raw,
        (shape((144, 128), BF16), shape((144, 128), BF16), shape((48, 128), BF16), tile),
        [pltpu.VMEM((384, 128), F32)] + copies_of(raw)[1:],
        space=HBM,
    )
    from_far = lax.ppermute(to_far, "rows", far)
    from_near = lax.ppermute(to_near, "rows", near)
    raw = [
        jnp.asarray(tap_matrix(), BF16),
        weight_in.reshape(9, 6, 128),
        bias_in.reshape(1, 128),
        weight_mid.reshape(9, 128, 128),
        jnp.transpose(time_mix, (1, 2, 0)),
        weight_out.T,
        jnp.asarray(spread_matrix(), BF16),
        blend,
        frame_slot,
        bias_out,
    ]
    w_in, w_mid, w_mix, w_out, maps, weights, shares, hot, offset = call(
        prepare_kernel,
        "prepare",
        [],
        raw,
        (
            shape((5, 256, 256), BF16),
            shape((256, 1536), BF16),
            shape((8, 256, 256), BF16),
            shape((8, 48, 256), BF16),
            shape((128, 896), BF16),
            shape((16, 128), F32),
            shape((32, 128), F32),
            shape((192, 384), BF16),
            shape((48, 128), F32),
        ),
        copies_of(raw[:7])[:7]
        + [pltpu.SMEM(a.shape, a.dtype) for a in raw[7:]]
        + [pltpu.SemaphoreType.DMA((10,))],
        flops=2 * 10**9,
        space=HBM,
    )
    rim, ask, pack = pl.pallas_call(
        middle_kernel,
        out_shape=(tile, shape((n_t, 24, 128), BF16), shape((3, 8, 16, 128), BF16)),
        in_specs=[VMEM] * 5,
        out_specs=(VMEM,) * 3,
        scratch_shapes=[pltpu.VMEM((384, 128), F32)],
        compiler_params=PARAMS,
        name="middle",
    )(own, from_near, from_far, base, weights)
    queue = lax.all_to_all(ask, "tm", 0, 0, tiled=True)
    ahead = lax.ppermute(pack, "tm", back)
    gain = gain_mid.reshape(1, 128)
    spatial, lifted_ahead = call(
        own_kernel,
        "own",
        [],
        [hot, own, rim, queue, gain, w_in, w_mid, maps],
        (shape((4, 16, 128, 256), BF16), shape((64, 384), F32)),
        network_scratch(16),
        flops=10**10,
    )
    send, next_half = call(
        late_kernel,
        "late",
        [],
        [offset, ahead, lifted_ahead, gain, w_in, w_mid, maps, w_mix, w_out, spatial],
        (shape((3, 8, 8, 128), BF16), shape((3, 8, 8, 128), F32)),
        network_scratch(8) + [pltpu.VMEM((4, 8, 128, 256), BF16)] + PICTURES,
        flops=10**10,
    )
    arrived = lax.ppermute(send, "tm", forth)
    (mine,) = call(
        early_kernel,
        "early",
        [],
        [offset, shares, maps, w_mix, w_out, spatial, next_half],
        (shape((3, 16, 8, 128), F32),),
        PICTURES,
        flops=5 * 10**9,
    )
    (out,) = call(join_kernel, "join", [], [mine, arrived], (shape((3, 16, 8, 128), F32),))
    return out


def solution(mesh):
    return jax.shard_map(
        body,
        mesh=mesh,
        in_specs=(
            P(None, "tm", "rows", None),
            P("tm", None, "rows", None),
            P(),
            P("tm", None),
            P(),
            P(),
            P(),
            P(),
            P(),
            P(),
            P(),
        ),
        out_specs=P(None, "tm", "rows", None),
        check_vma=False,
    )
```

```python
import functools

import jax
import jax.numpy as jnp
import numpy as np
from jax import lax
from jax.experimental import pallas as pl
from jax.experimental.pallas import tpu as pltpu
from jax.sharding import PartitionSpec as P

BF16 = jnp.bfloat16
F32 = jnp.float32
NT = (((1,), (1,)), ((), ()))
VMEM = pl.BlockSpec(memory_space=pltpu.VMEM)
HBM = pl.BlockSpec(memory_space=pltpu.HBM)
SMEM = pl.BlockSpec(memory_space=pltpu.SMEM)
PARAMS = pltpu.CompilerParams(vmem_limit_bytes=24 * 2**20)


def tap_matrix():
    m = np.zeros((5, 2, 256, 72), np.float32)
    for q in range(5):
        for e in range(2):
            for dr in range(3):
                row = 2 * q + e - 2 + dr
                for dv in range(3):
                    for ch in range(6):
                        tap = (dr * 3 + dv) * 8 + ch
                        if ch < 3:
                            if 0 <= row < 8:
                                k = ch * 8 + row
                            else:
                                k = 24 + ch * 8 + (row + 2 if row < 0 else row - 6)
                            m[q, e, dv * 80 + k, tap] += 1
                        else:
                            br = 0 if row < 0 else (1 if row < 8 else 2)
                            m[q, e, dv * 80 + 48 + br * 8 + ch - 3, tap] += 1
                            m[q, e, dv * 80 + 48 + br * 8 + ch, tap] += 1
    return m.reshape(10, 256, 72)


def spread_matrix():
    m = np.zeros((496, 256), np.float32)
    m[240 + np.arange(256) // 16, np.arange(256)] = 1
    return m


def iota(shape, dim):
    return lax.broadcasted_iota(jnp.int32, shape, dim)


def fetch(sources, targets, sems):
    copies = [
        pltpu.make_async_copy(source, target, sems.at[i])
        for i, (source, target) in enumerate(zip(sources, targets))
    ]
    for copy in copies:
        copy.start()
    for copy in copies:
        copy.wait()


def pack_kernel(own_hbm, queue_hbm, to_near, to_far, base, own, wide, queue, sems):
    fetch([own_hbm, queue_hbm], [own, queue], sems)
    wide[...] = own[...].astype(F32).reshape(384, 128)
    put = (iota((16, 384), 0) == iota((16, 384), 1) % 128 - iota((16, 384), 1) // 128 * 16).astype(BF16)
    placed = jnp.dot(queue[...].reshape(48, 16), put, preferred_element_type=F32)
    even = lax.rem(lax.axis_index("rows"), 2) == 0
    parts = [
        (wide[pl.ds(6, 48, stride=8), :], wide[pl.ds(0, 48, stride=8), :]),
        (wide[pl.ds(7, 48, stride=8), :], wide[pl.ds(1, 48, stride=8), :]),
        (placed[:, 0:128], placed[:, 256:384]),
    ]
    for k, (down, up) in enumerate(parts):
        to_near[k * 48 : (k + 1) * 48, :] = jnp.where(even, down, up).astype(BF16)
        to_far[k * 48 : (k + 1) * 48, :] = jnp.where(even, up, down).astype(BF16)
    base[...] = placed[:, 128:256].astype(BF16)


def middle_kernel(own, near, far, base, weights, rim, ask, back, both):
    both[...] = jnp.zeros_like(both)
    even = lax.rem(lax.axis_index("rows"), 2) == 0
    for k in range(2):
        x = near[k * 48 : (k + 1) * 48, :].astype(F32)
        y = far[k * 48 : (k + 1) * 48, :].astype(F32)
        both[pl.ds(k, 48, stride=8), :] = jnp.where(even, y, x)
        both[pl.ds(k + 2, 48, stride=8), :] = jnp.where(even, x, y)
    x = both[...].reshape(3, 16, 8, 128)
    rim[...] = x.astype(BF16)
    three = near[96:144, :].astype(F32) + far[96:144, :].astype(F32)
    three = three + base[...].astype(F32)
    three = (three[:24] + pltpu.roll(three[24:], 64, 1)).astype(BF16)
    for i in range(ask.shape[0]):
        ask[i] = three
    row = iota((8, 128), 0)
    for ch in range(3):
        for f in range(8):
            y = jnp.where(row == 6, weights[f : f + 1, :], x[ch, f])
            y = jnp.where(row == 7, weights[f + 8 : f + 9, :], y)
            both_rows = jnp.concatenate([own[ch, f].astype(F32), y], axis=0)
            back[ch, f] = both_rows.astype(BF16)


def selection(frame_slot):
    j = iota((8, 384), 0)
    lane = iota((8, 384), 1)
    start = lax.axis_index("tm") * 16
    hot = []
    for f in range(24):
        slot = frame_slot[jnp.minimum(start + f, 127)]
        row = j % 3 * 16 + slot % 16
        place = slot // 16 * 24 + jnp.where(row < 24, row, row + 168)
        hot.append(jnp.where((lane == place) & (j < 6), 1.0, 0.0))
    return jnp.concatenate(hot, axis=0).astype(BF16)


def blend_shares(blend):
    t = lax.axis_index("tm")
    has_prev = jnp.where(t > 0, 1.0, 0.0)
    has_next = jnp.where(t < lax.axis_size("tm") - 1, 1.0, 0.0)
    row = iota((16, 128), 0)
    lead = jnp.zeros((16, 128), F32)
    trail = jnp.zeros((16, 128), F32)
    for f in range(16):
        lead = jnp.where(row == f, blend[0, f].astype(F32), lead)
        trail = jnp.where(row == f, blend[1, f].astype(F32), trail)
    raw = jnp.concatenate([lead[0:8], trail[0:8]], axis=0)
    lead = jnp.where(row < 8, lead, lead * has_next)
    trail = jnp.where(row < 8, trail * has_prev, trail)
    total = lead + trail
    return raw, jnp.concatenate([lead / total, trail / total], axis=0)


def prepare_kernel(*refs):
    sources, made, targets, sems = refs[:10], refs[10:19], refs[19:29], refs[29]
    fetch(sources, targets, sems)
    taps, win, bias, wmid, mix, wout, over, blend, frame_slot, bias_out = targets
    w_in, w_mid, w_mix, w_out, maps, weights, shares, hot, offset = made
    weights[...], shares[...] = blend_shares(blend)
    hot[...] = selection(frame_slot)
    for o in range(3):
        offset[o * 16 : (o + 1) * 16, :] = jnp.zeros((16, 128), F32) + bias_out[o]
    col = iota((128, 384), 0)
    lane = iota((128, 384), 1)
    pixel = lane & 127
    maps[:, 0:384] = (col == (pixel & 15) * 8 + (pixel >> 4) + (lane >> 7) - 1).astype(BF16)
    maps[:, 384:768] = (col == (lane >> 7) * 16 + (pixel >> 3)).astype(BF16)
    col = iota((128, 128), 0)
    maps[:, 768:896] = (iota((128, 128), 1) == (col & 15) * 8 + (col >> 4)).astype(BF16)
    k = iota((256, 128), 0)
    low = (k % 80 >= 48) & (k % 80 < 72) & (k % 8 >= 3) & (k % 8 < 6) & (k < 240)
    b = bias[...]
    b0 = b.astype(BF16).astype(F32)
    b1 = (b - b0).astype(BF16).astype(F32)
    b2 = b - b0 - b1
    pad = jnp.zeros((2, 128), F32)
    w = [jnp.concatenate([win[i].astype(F32), pad], axis=0) for i in range(9)]
    w = jnp.concatenate(w, axis=0).astype(BF16)
    for q in range(5):
        for e in range(2):
            v = jnp.dot(taps[2 * q + e], w, preferred_element_type=F32)
            v = jnp.where(low, v - v.astype(BF16).astype(F32), v)
            v = jnp.where(k == 152, b0, jnp.where(k == 153, b1, jnp.where(k == 154, b2, v)))
            w_in[q, :, e * 128 : (e + 1) * 128] = v.astype(BF16)
    none = jnp.zeros((128, 384), BF16)
    w_mid[0:128, 1152:1536] = none
    w_mid[128:256, 0:384] = none
    for dr in range(3):
        for dv in range(3):
            t = wmid[dr * 3 + dv].T
            for e in range(2):
                tap = (dr + e) * 3 + dv
                w_mid[e * 128 : (e + 1) * 128, tap * 128 : (tap + 1) * 128] = t
    flat = mix[...].reshape(256, 128)
    flat = jnp.concatenate([flat[:128].T, flat[128:].T], axis=1)
    same = iota((128, 256), 0) % 16 == iota((128, 256), 1) % 16
    for p in range(16):
        t = jnp.dot(flat, over[240 - 16 * p : 496 - 16 * p, :], preferred_element_type=F32)
        t = jnp.where(same, t, 0.0).astype(BF16)
        for g in range(8):
            w_mix[g, p * 16 : (p + 1) * 16, :] = t[g * 16 : (g + 1) * 16, :]
    own = iota((16, 256), 0) == iota((16, 256), 1) // 16
    wo = jnp.concatenate([wout[...].astype(F32), jnp.zeros((5, 128), F32)], axis=0).astype(BF16)
    for g in range(8):
        pick = (iota((128, 256), 0) == g * 16 + iota((128, 256), 1) % 16).astype(BF16)
        t = jnp.dot(wo, pick, preferred_element_type=F32)
        for o in range(3):
            w_out[g, o * 16 : (o + 1) * 16, :] = jnp.where(own, t[o : o + 1, :], 0.0).astype(BF16)


def lift(hot, queue, maps):
    rows = queue[...].astype(F32).reshape(192, 128)
    rows = jnp.concatenate([rows, pltpu.roll(rows, 64, 1)], axis=0).astype(BF16)
    chosen = jnp.dot(hot[...], rows, preferred_element_type=F32).astype(BF16)
    return jnp.dot(chosen, maps[:, 384:768], preferred_element_type=F32)


def tiles_of(own, rim, lifted):
    tiles = own + rim + [lifted[:, br * 128 : (br + 1) * 128] for br in range(3)]
    return jnp.concatenate(tiles + [jnp.ones((8, 128), F32)], axis=0).astype(BF16)


def stage(inputs, at, frames, maps):
    x = jnp.concatenate(frames, axis=0)
    x = jnp.dot(x, maps[:, 0:384], preferred_element_type=F32).astype(BF16)
    for f in range(len(frames)):
        for dv in range(3):
            inputs[at + f, dv * 80 : (dv + 1) * 80, :] = x[
                f * 80 : (f + 1) * 80, dv * 128 : (dv + 1) * 128
            ]
        inputs[at + f, 240:256, :] = jnp.zeros((16, 128), BF16)


def gains(gain):
    r = lax.axis_index("rows")
    top = jnp.where(r > 0, 0.5, 0.0)
    bottom = jnp.where(r < lax.axis_size("rows") - 1, 0.5, 0.0)
    g = gain[...]
    out = []
    for q in range(5):
        first = g * (top if q == 0 else 0.5)
        second = g * (bottom if q == 4 else 0.5)
        out.append(jnp.concatenate([first, second], axis=1))
    return out


def spread_inputs(inputs, pair):
    return jnp.concatenate([inputs[pair * 2 + b].T for b in range(2)], axis=0)


def norm_act(h, gain, act, q):
    sq = h * h
    parts = []
    for e in range(2):
        lanes = slice(e * 128, (e + 1) * 128)
        ss = jnp.sum(sq[:, lanes], axis=1, keepdims=True)
        scale = lax.rsqrt(ss * (1 / 128) + 1e-6)
        u = h[:, lanes] * scale * gain[:, lanes]
        parts.append(u * jnp.tanh(u) + u)
    s = iota((16, 128), 0)
    for e in range(2):
        a = parts[e].reshape(2, 128, 128)
        act[:, 2 * q + e, 1:9] = a.astype(BF16).reshape(2, 8, 16, 128)
        for b in range(2):
            left = jnp.where(s == 0, 0.0, pltpu.roll(a[b, 112:128], 1, 0))
            right = jnp.where(s == 15, 0.0, pltpu.roll(a[b, 0:16], 15, 0))
            act[b, 2 * q + e, 0] = left.astype(BF16)
            act[b, 2 * q + e, 9] = right.astype(BF16)


def mid_conv(act, w_mid, spatial, at, i):
    frames = []
    for b in range(2):
        taps = [
            act[b, 2 * i + dr, dv : dv + 8].reshape(128, 128) for dr in range(4) for dv in range(3)
        ]
        frames.append(jnp.concatenate(taps, axis=1))
    x = jnp.concatenate(frames, axis=0)
    y = lax.dot_general(w_mid[...], x, NT, preferred_element_type=F32).astype(BF16)
    for b in range(2):
        for e in range(2):
            spatial[i, at + b, :, e * 128 : (e + 1) * 128] = y[
                e * 128 : (e + 1) * 128, b * 128 : (b + 1) * 128
            ]


def network(inputs, pairs, frame, maps, w_in, w_mid, gain, act0, act1, spatial):
    def step(done, pair, todo, following):
        if todo is not None:
            depth = spread_inputs(inputs, following)
            h = jnp.dot(depth, w_in[0], preferred_element_type=F32)
        for q in range(5):
            if done is not None and q < 4:
                mid_conv(done, w_mid, spatial, pair * 2, q)
            if todo is not None:
                now = h
                if q < 4:
                    h = jnp.dot(depth, w_in[q + 1], preferred_element_type=F32)
                norm_act(now, gain[q], todo, q)

    for part in range(pairs // 2):
        stage(inputs, part * 4, [frame(part * 4 + f) for f in range(4)], maps)
    acts = [act0, act1]
    step(None, None, act0, 0)
    for p in range(pairs):
        step(acts[p % 2], p, acts[1 - p % 2] if p < pairs - 1 else None, p + 1)


def predict(halves, w_mix, w_out, offset, total, first_half=None):
    def mixed(i, g):
        rows = slice(g * 16, (g + 1) * 16)
        x = [ref[i, at : at + 8, rows, :].reshape(128, 256) for ref, at in halves]
        x = jnp.concatenate(x, axis=0)
        return jnp.dot(w_mix[g], x, preferred_element_type=F32) + x.astype(F32)

    order = [(i, g) for i in range(4) for g in range(8)]
    queued = [mixed(*order[n]) for n in range(3)]
    for n, (i, g) in enumerate(order):
        now = queued.pop(0)
        if n + 3 < len(order):
            queued.append(mixed(*order[n + 3]))
        h = 0.5 * now
        outer = (h * jnp.tanh(h) + h).astype(BF16)
        lanes = slice(0, 256)
        if first_half is not None:
            first_half[i, g] = outer[:128]
            outer = outer[128:]
            lanes = slice(128, 256)
        if g % 2 == 0:
            held = outer
            continue
        w = jnp.concatenate([w_out[g - 1, :, lanes], w_out[g, :, lanes]], axis=1)
        p = jnp.dot(w, jnp.concatenate([held, outer], axis=0), preferred_element_type=F32)
        acc = p if g == 1 else acc + p
        if g == 7:
            store(acc, offset, total, i)


def store(acc, offset, total, i):
    for e in range(2):
        total[2 * i + e] = acc[:, e * 128 : (e + 1) * 128] + offset[...]


def project_half(first_half, w_out, offset, total):
    for i in range(4):
        for g in range(0, 8, 2):
            w = jnp.concatenate([w_out[g, :, 0:128], w_out[g + 1, :, 0:128]], axis=1)
            x = first_half[i, g : g + 2].reshape(256, 256)
            p = jnp.dot(w, x, preferred_element_type=F32)
            acc = p if g == 0 else acc + p
        store(acc, offset, total, i)


def unorder(total, maps, rows):
    x = total[...].reshape(384, 128)
    x0 = x.astype(BF16)
    r = x - x0.astype(F32)
    x1 = r.astype(BF16)
    x2 = (r - x1.astype(F32)).astype(BF16)
    y = [jnp.dot(part, maps[:, 768:896], preferred_element_type=F32) for part in (x0, x1, x2)]
    rows[...] = y[0] + (y[1] + y[2])


def picture(rows, o, f):
    return rows[pl.ds(o * 16 + f, 8, stride=48), :]


def own_kernel(
    hot, own, rim, queue, gain, w_in, w_mid, maps, spatial, lifted_ahead, inputs, act0, act1
):
    lifted = lift(hot, queue, maps)
    lifted_ahead[...] = lifted[128:]

    def frame(f):
        noisy = [own[ch, f].astype(F32) for ch in range(3)]
        edge = [rim[ch, f].astype(F32) for ch in range(3)]
        return tiles_of(noisy, edge, lifted[f * 8 : f * 8 + 8])

    network(inputs, 8, frame, maps, w_in, w_mid, gains(gain), act0, act1, spatial)


def late_kernel(
    offset, ahead, lifted, gain, w_in, w_mid, maps, w_mix, w_out, own,
    send, kept, inputs, act0, act1, spatial, total, rows,
):
    def frame(f):
        x = [ahead[ch, f].astype(F32) for ch in range(3)]
        noisy, edge = [tile[:8] for tile in x], [tile[8:] for tile in x]
        return tiles_of(noisy, edge, lifted[f * 8 : f * 8 + 8, :])

    network(inputs, 4, frame, maps, w_in, w_mid, gains(gain), act0, act1, spatial)
    predict([(own, 8), (spatial, 0)], w_mix, w_out, offset, total, kept)
    unorder(total, maps, rows)
    for f in range(8):
        w = ahead[0, f].astype(F32)
        share = w[15:16] / jnp.maximum(w[14:15] + w[15:16], 1.0)
        for o in range(3):
            send[o, f] = (picture(rows, o, f + 8) * share).astype(BF16)


def early_kernel(
    offset, shares, maps, w_mix, w_out, own, kept, mine, total, rows, total_next, rows_next
):
    project_half(kept, w_out, offset, total_next)
    unorder(total_next, maps, rows_next)
    predict([(own, 0), (own, 8)], w_mix, w_out, offset, total)
    unorder(total, maps, rows)
    for f in range(16):
        lead, trail = shares[f : f + 1, :], shares[f + 16 : f + 17, :]
        for o in range(3):
            if f < 8:
                mine[o, f] = picture(rows, o, f) * lead
            else:
                mine[o, f] = picture(rows_next, o, f - 8) * lead + picture(rows, o, f) * trail


def join_kernel(mine, arrived, out):
    out[:, 0:8] = mine[:, 0:8] + arrived[...].astype(F32)
    out[:, 8:16] = mine[:, 8:16]


def network_scratch(frames):
    act = pltpu.VMEM((2, 10, 10, 16, 128), BF16)
    return [pltpu.VMEM((frames, 256, 128), BF16), act, act]


PICTURES = [pltpu.VMEM((8, 48, 128), F32), pltpu.VMEM((384, 128), F32)]


def shape(dims, kind):
    return jax.ShapeDtypeStruct(dims, kind)


def call(kernel, name, scalars, arrays, outs, scratch_shapes=(), flops=10**8, space=VMEM):
    if space is HBM:
        arrays = [pltpu.with_memory_space_constraint(a, pltpu.HBM) for a in arrays]
    return pl.pallas_call(
        kernel,
        out_shape=outs,
        in_specs=[SMEM] * len(scalars) + [space] * len(arrays),
        out_specs=tuple(VMEM for _ in outs),
        scratch_shapes=list(scratch_shapes),
        compiler_params=PARAMS,
        cost_estimate=pl.CostEstimate(flops=flops, bytes_accessed=10**6, transcendentals=0),
        name=name,
    )(*scalars, *arrays)


def copies_of(arrays):
    return [pltpu.VMEM(a.shape, a.dtype) for a in arrays] + [pltpu.SemaphoreType.DMA((len(arrays),))]


def body(
    noisy_frames, base_queue, frame_slot, blend_weight, weight_in, bias_in, gain_mid, weight_mid,
    time_mix, weight_out, bias_out,
):
    n_t = lax.axis_size("tm")
    n_r = lax.axis_size("rows")
    near = [(i, i ^ 1) for i in range(n_r)]
    far = [(i, (i - 1 ^ 1) + 1) for i in range(1, n_r - 1)]
    back = [(i + 1, i) for i in range(n_t - 1)]
    forth = [(i, i + 1) for i in range(n_t - 1)]
    blend = blend_weight.T
    tile = shape((3, 16, 8, 128), BF16)

    raw = [noisy_frames, jnp.transpose(base_queue[:, :, 0, :], (1, 0, 2))]
    to_near, to_far, base, own = call(
        pack_kernel,
        "pack",
        [],
        raw,
        (shape((144, 128), BF16), shape((144, 128), BF16), shape((48, 128), BF16), tile),
        [pltpu.VMEM((384, 128), F32)] + copies_of(raw)[1:],
        space=HBM,
    )
    from_far = lax.ppermute(to_far, "rows", far)
    from_near = lax.ppermute(to_near, "rows", near)
    raw = [
        jnp.asarray(tap_matrix(), BF16),
        weight_in.reshape(9, 6, 128),
        bias_in.reshape(1, 128),
        weight_mid.reshape(9, 128, 128),
        jnp.transpose(time_mix, (1, 2, 0)),
        weight_out.T,
        jnp.asarray(spread_matrix(), BF16),
        blend,
        frame_slot,
        bias_out,
    ]
    w_in, w_mid, w_mix, w_out, maps, weights, shares, hot, offset = call(
        prepare_kernel,
        "prepare",
        [],
        raw,
        (
            shape((5, 256, 256), BF16),
            shape((256, 1536), BF16),
            shape((8, 256, 256), BF16),
            shape((8, 48, 256), BF16),
            shape((128, 896), BF16),
            shape((16, 128), F32),
            shape((32, 128), F32),
            shape((192, 384), BF16),
            shape((48, 128), F32),
        ),
        copies_of(raw[:7])[:7]
        + [pltpu.SMEM(a.shape, a.dtype) for a in raw[7:]]
        + [pltpu.SemaphoreType.DMA((10,))],
        flops=2 * 10**9,
        space=HBM,
    )
    rim, ask, pack = pl.pallas_call(
        middle_kernel,
        out_shape=(tile, shape((n_t, 24, 128), BF16), shape((3, 8, 16, 128), BF16)),
        in_specs=[VMEM] * 5,
        out_specs=(VMEM,) * 3,
        scratch_shapes=[pltpu.VMEM((384, 128), F32)],
        compiler_params=PARAMS,
        name="middle",
    )(own, from_near, from_far, base, weights)
    queue = lax.all_to_all(ask, "tm", 0, 0, tiled=True)
    ahead = lax.ppermute(pack, "tm", back)
    gain = gain_mid.reshape(1, 128)
    spatial, lifted_ahead = call(
        own_kernel,
        "own",
        [],
        [hot, own, rim, queue, gain, w_in, w_mid, maps],
        (shape((4, 16, 128, 256), BF16), shape((64, 384), F32)),
        network_scratch(16),
        flops=10**10,
    )
    send, kept = call(
        late_kernel,
        "late",
        [],
        [offset, ahead, lifted_ahead, gain, w_in, w_mid, maps, w_mix, w_out, spatial],
        (shape((3, 8, 8, 128), BF16), shape((4, 8, 128, 256), BF16)),
        network_scratch(8) + [pltpu.VMEM((4, 8, 128, 256), BF16)] + PICTURES,
        flops=10**10,
    )
    arrived = lax.ppermute(send, "tm", forth)
    (mine,) = call(
        early_kernel,
        "early",
        [],
        [offset, shares, maps, w_mix, w_out, spatial, kept],
        (shape((3, 16, 8, 128), F32),),
        PICTURES + PICTURES,
        flops=5 * 10**9,
    )
    (out,) = call(join_kernel, "join", [], [mine, arrived], (shape((3, 16, 8, 128), F32),))
    return out


def solution(mesh):
    return jax.shard_map(
        body,
        mesh=mesh,
        in_specs=(
            P(None, "tm", "rows", None),
            P("tm", None, "rows", None),
            P(),
            P("tm", None),
            P(),
            P(),
            P(),
            P(),
            P(),
            P(),
            P(),
        ),
        out_specs=P(None, "tm", "rows", None),
        check_vma=False,
    )
```

```python
import functools

import jax
import jax.numpy as jnp
import numpy as np
from jax import lax
from jax.experimental import pallas as pl
from jax.experimental.pallas import tpu as pltpu
from jax.sharding import PartitionSpec as P

BF16 = jnp.bfloat16
F32 = jnp.float32
NT = (((1,), (1,)), ((), ()))
VMEM = pl.BlockSpec(memory_space=pltpu.VMEM)
HBM = pl.BlockSpec(memory_space=pltpu.HBM)
SMEM = pl.BlockSpec(memory_space=pltpu.SMEM)
PARAMS = pltpu.CompilerParams(vmem_limit_bytes=24 * 2**20)


def tap_matrix():
    m = np.zeros((5, 2, 256, 72), np.float32)
    for q in range(5):
        for e in range(2):
            for dr in range(3):
                row = 2 * q + e - 2 + dr
                for dv in range(3):
                    for ch in range(6):
                        tap = (dr * 3 + dv) * 8 + ch
                        if ch < 3:
                            if 0 <= row < 8:
                                k = ch * 8 + row
                            else:
                                k = 24 + ch * 8 + (row + 2 if row < 0 else row - 6)
                            m[q, e, dv * 80 + k, tap] += 1
                        else:
                            br = 0 if row < 0 else (1 if row < 8 else 2)
                            m[q, e, dv * 80 + 48 + br * 8 + ch - 3, tap] += 1
                            m[q, e, dv * 80 + 48 + br * 8 + ch, tap] += 1
    return m.reshape(10, 256, 72)


def spread_matrix():
    m = np.zeros((496, 256), np.float32)
    m[240 + np.arange(256) // 16, np.arange(256)] = 1
    return m


def iota(shape, dim):
    return lax.broadcasted_iota(jnp.int32, shape, dim)


def fetch(sources, targets, sems):
    copies = [
        pltpu.make_async_copy(source, target, sems.at[i])
        for i, (source, target) in enumerate(zip(sources, targets))
    ]
    for copy in copies:
        copy.start()
    for copy in copies:
        copy.wait()


def pack_kernel(own_hbm, queue_hbm, to_near, to_far, base, own, wide, queue, sems):
    fetch([own_hbm, queue_hbm], [own, queue], sems)
    wide[...] = own[...].astype(F32).reshape(384, 128)
    put = (iota((16, 384), 0) == iota((16, 384), 1) % 128 - iota((16, 384), 1) // 128 * 16).astype(BF16)
    placed = jnp.dot(queue[...].reshape(48, 16), put, preferred_element_type=F32)
    even = lax.rem(lax.axis_index("rows"), 2) == 0
    parts = [
        (wide[pl.ds(6, 48, stride=8), :], wide[pl.ds(0, 48, stride=8), :]),
        (wide[pl.ds(7, 48, stride=8), :], wide[pl.ds(1, 48, stride=8), :]),
        (placed[:, 0:128], placed[:, 256:384]),
    ]
    for k, (down, up) in enumerate(parts):
        to_near[k * 48 : (k + 1) * 48, :] = jnp.where(even, down, up).astype(BF16)
        to_far[k * 48 : (k + 1) * 48, :] = jnp.where(even, up, down).astype(BF16)
    base[...] = placed[:, 128:256].astype(BF16)


def middle_kernel(own, near, far, base, weights, rim, ask, back, both):
    both[...] = jnp.zeros_like(both)
    even = lax.rem(lax.axis_index("rows"), 2) == 0
    for k in range(2):
        x = near[k * 48 : (k + 1) * 48, :].astype(F32)
        y = far[k * 48 : (k + 1) * 48, :].astype(F32)
        both[pl.ds(k, 48, stride=8), :] = jnp.where(even, y, x)
        both[pl.ds(k + 2, 48, stride=8), :] = jnp.where(even, x, y)
    x = both[...].reshape(3, 16, 8, 128)
    rim[...] = x.astype(BF16)
    three = near[96:144, :].astype(F32) + far[96:144, :].astype(F32)
    three = three + base[...].astype(F32)
    three = (three[:24] + pltpu.roll(three[24:], 64, 1)).astype(BF16)
    for i in range(ask.shape[0]):
        ask[i] = three
    row = iota((8, 128), 0)
    for ch in range(3):
        for f in range(8):
            y = jnp.where(row == 6, weights[f : f + 1, :], x[ch, f])
            y = jnp.where(row == 7, weights[f + 8 : f + 9, :], y)
            both_rows = jnp.concatenate([own[ch, f].astype(F32), y], axis=0)
            back[ch, f] = both_rows.astype(BF16)


def selection(frame_slot):
    j = iota((8, 384), 0)
    lane = iota((8, 384), 1)
    start = lax.axis_index("tm") * 16
    hot = []
    for f in range(24):
        slot = frame_slot[jnp.minimum(start + f, 127)]
        row = j % 3 * 16 + slot % 16
        place = slot // 16 * 24 + jnp.where(row < 24, row, row + 168)
        hot.append(jnp.where((lane == place) & (j < 6), 1.0, 0.0))
    return jnp.concatenate(hot, axis=0).astype(BF16)


def blend_shares(blend):
    t = lax.axis_index("tm")
    has_prev = jnp.where(t > 0, 1.0, 0.0)
    has_next = jnp.where(t < lax.axis_size("tm") - 1, 1.0, 0.0)
    row = iota((16, 128), 0)
    lead = jnp.zeros((16, 128), F32)
    trail = jnp.zeros((16, 128), F32)
    for f in range(16):
        lead = jnp.where(row == f, blend[0, f].astype(F32), lead)
        trail = jnp.where(row == f, blend[1, f].astype(F32), trail)
    raw = jnp.concatenate([lead[0:8], trail[0:8]], axis=0)
    lead = jnp.where(row < 8, lead, lead * has_next)
    trail = jnp.where(row < 8, trail * has_prev, trail)
    total = lead + trail
    return raw, jnp.concatenate([lead / total, trail / total], axis=0)


def prepare_kernel(*refs):
    sources, made, targets, sems = refs[:10], refs[10:19], refs[19:29], refs[29]
    fetch(sources, targets, sems)
    taps, win, bias, wmid, mix, wout, over, blend, frame_slot, bias_out = targets
    w_in, w_mid, w_mix, w_out, maps, weights, shares, hot, offset = made
    weights[...], shares[...] = blend_shares(blend)
    hot[...] = selection(frame_slot)
    for o in range(3):
        offset[o * 16 : (o + 1) * 16, :] = jnp.zeros((16, 128), F32) + bias_out[o]
    col = iota((128, 384), 0)
    lane = iota((128, 384), 1)
    pixel = lane & 127
    maps[:, 0:384] = (col == (pixel & 15) * 8 + (pixel >> 4) + (lane >> 7) - 1).astype(BF16)
    maps[:, 384:768] = (col == (lane >> 7) * 16 + (pixel >> 3)).astype(BF16)
    col = iota((128, 128), 0)
    maps[:, 768:896] = (iota((128, 128), 1) == (col & 15) * 8 + (col >> 4)).astype(BF16)
    k = iota((256, 128), 0)
    low = (k % 80 >= 48) & (k % 80 < 72) & (k % 8 >= 3) & (k % 8 < 6) & (k < 240)
    b = bias[...]
    b0 = b.astype(BF16).astype(F32)
    b1 = (b - b0).astype(BF16).astype(F32)
    b2 = b - b0 - b1
    pad = jnp.zeros((2, 128), F32)
    w = [jnp.concatenate([win[i].astype(F32), pad], axis=0) for i in range(9)]
    w = jnp.concatenate(w, axis=0).astype(BF16)
    for q in range(5):
        for e in range(2):
            v = jnp.dot(taps[2 * q + e], w, preferred_element_type=F32)
            v = jnp.where(low, v - v.astype(BF16).astype(F32), v)
            v = jnp.where(k == 152, b0, jnp.where(k == 153, b1, jnp.where(k == 154, b2, v)))
            w_in[q, :, e * 128 : (e + 1) * 128] = v.astype(BF16)
    none = jnp.zeros((128, 384), BF16)
    w_mid[0:128, 1152:1536] = none
    w_mid[128:256, 0:384] = none
    for dr in range(3):
        for dv in range(3):
            t = wmid[dr * 3 + dv].T
            for e in range(2):
                tap = (dr + e) * 3 + dv
                w_mid[e * 128 : (e + 1) * 128, tap * 128 : (tap + 1) * 128] = t
    flat = mix[...].reshape(256, 128)
    flat = jnp.concatenate([flat[:128].T, flat[128:].T], axis=1)
    same = iota((128, 256), 0) % 16 == iota((128, 256), 1) % 16
    for p in range(16):
        t = jnp.dot(flat, over[240 - 16 * p : 496 - 16 * p, :], preferred_element_type=F32)
        t = jnp.where(same, t, 0.0).astype(BF16)
        for g in range(8):
            w_mix[g, p * 16 : (p + 1) * 16, :] = t[g * 16 : (g + 1) * 16, :]
    own = iota((16, 256), 0) == iota((16, 256), 1) // 16
    wo = jnp.concatenate([wout[...].astype(F32), jnp.zeros((5, 128), F32)], axis=0).astype(BF16)
    for g in range(8):
        pick = (iota((128, 256), 0) == g * 16 + iota((128, 256), 1) % 16).astype(BF16)
        t = jnp.dot(wo, pick, preferred_element_type=F32)
        for o in range(3):
            w_out[g, o * 16 : (o + 1) * 16, :] = jnp.where(own, t[o : o + 1, :], 0.0).astype(BF16)


def lift(hot, queue, maps):
    rows = queue[...].astype(F32).reshape(192, 128)
    rows = jnp.concatenate([rows, pltpu.roll(rows, 64, 1)], axis=0).astype(BF16)
    chosen = jnp.dot(hot[...], rows, preferred_element_type=F32).astype(BF16)
    return jnp.dot(chosen, maps[:, 384:768], preferred_element_type=F32)


def tiles_of(own, rim, lifted):
    tiles = own + rim + [lifted[:, br * 128 : (br + 1) * 128] for br in range(3)]
    return jnp.concatenate(tiles + [jnp.ones((8, 128), F32)], axis=0).astype(BF16)


def stage(inputs, at, frames, maps):
    x = jnp.concatenate(frames, axis=0)
    x = jnp.dot(x, maps[:, 0:384], preferred_element_type=F32).astype(BF16)
    for f in range(len(frames)):
        for dv in range(3):
            inputs[at + f, dv * 80 : (dv + 1) * 80, :] = x[
                f * 80 : (f + 1) * 80, dv * 128 : (dv + 1) * 128
            ]
        inputs[at + f, 240:256, :] = jnp.zeros((16, 128), BF16)


def gains(gain):
    r = lax.axis_index("rows")
    top = jnp.where(r > 0, 0.5, 0.0)
    bottom = jnp.where(r < lax.axis_size("rows") - 1, 0.5, 0.0)
    g = gain[...]
    out = []
    for q in range(5):
        first = g * (top if q == 0 else 0.5)
        second = g * (bottom if q == 4 else 0.5)
        out.append(jnp.concatenate([first, second], axis=1))
    return out


def spread_inputs(inputs, pair):
    return jnp.concatenate([inputs[pair * 2 + b].T for b in range(2)], axis=0)


def norm_act(h, gain, act, q):
    sq = h * h
    parts = []
    for e in range(2):
        lanes = slice(e * 128, (e + 1) * 128)
        ss = jnp.sum(sq[:, lanes], axis=1, keepdims=True)
        scale = lax.rsqrt(ss * (1 / 128) + 1e-6)
        u = h[:, lanes] * scale * gain[:, lanes]
        parts.append(u * jnp.tanh(u) + u)
    s = iota((16, 128), 0)
    for e in range(2):
        a = parts[e].reshape(2, 128, 128)
        act[:, 2 * q + e, 1:9] = a.astype(BF16).reshape(2, 8, 16, 128)
        for b in range(2):
            left = jnp.where(s == 0, 0.0, pltpu.roll(a[b, 112:128], 1, 0))
            right = jnp.where(s == 15, 0.0, pltpu.roll(a[b, 0:16], 15, 0))
            act[b, 2 * q + e, 0] = left.astype(BF16)
            act[b, 2 * q + e, 9] = right.astype(BF16)


def mid_conv(act, w_mid, spatial, at, i):
    frames = []
    for b in range(2):
        taps = [
            act[b, 2 * i + dr, dv : dv + 8].reshape(128, 128) for dr in range(4) for dv in range(3)
        ]
        frames.append(jnp.concatenate(taps, axis=1))
    x = jnp.concatenate(frames, axis=0)
    y = lax.dot_general(w_mid[...], x, NT, preferred_element_type=F32).astype(BF16)
    for b in range(2):
        for e in range(2):
            spatial[i, at + b, :, e * 128 : (e + 1) * 128] = y[
                e * 128 : (e + 1) * 128, b * 128 : (b + 1) * 128
            ]


def network(inputs, pairs, frame, maps, w_in, w_mid, gain, act0, act1, spatial):
    def step(done, pair, todo, following):
        if todo is not None:
            depth = spread_inputs(inputs, following)
            h = jnp.dot(depth, w_in[0], preferred_element_type=F32)
        for q in range(5):
            if done is not None and q < 4:
                mid_conv(done, w_mid, spatial, pair * 2, q)
            if todo is not None:
                now = h
                if q < 4:
                    h = jnp.dot(depth, w_in[q + 1], preferred_element_type=F32)
                norm_act(now, gain[q], todo, q)

    for part in range(pairs // 2):
        stage(inputs, part * 4, [frame(part * 4 + f) for f in range(4)], maps)
    acts = [act0, act1]
    step(None, None, act0, 0)
    for p in range(pairs):
        step(acts[p % 2], p, acts[1 - p % 2] if p < pairs - 1 else None, p + 1)


def predict(halves, w_mix, w_out, offset, total, first_half=None):
    def mixed(i, g):
        rows = slice(g * 16, (g + 1) * 16)
        x = [ref[i, at : at + 8, rows, :].reshape(128, 256) for ref, at in halves]
        x = jnp.concatenate(x, axis=0)
        return jnp.dot(w_mix[g], x, preferred_element_type=F32) + x.astype(F32)

    order = [(i, g) for i in range(4) for g in range(8)]
    queued = [mixed(*order[n]) for n in range(3)]
    for n, (i, g) in enumerate(order):
        now = queued.pop(0)
        if n + 3 < len(order):
            queued.append(mixed(*order[n + 3]))
        h = 0.5 * now
        outer = (h * jnp.tanh(h) + h).astype(BF16)
        lanes = slice(0, 256)
        if first_half is not None:
            first_half[i, g] = outer[:128]
            outer = outer[128:]
            lanes = slice(128, 256)
        if g % 2 == 0:
            held = outer
            continue
        w = jnp.concatenate([w_out[g - 1, :, lanes], w_out[g, :, lanes]], axis=1)
        p = jnp.dot(w, jnp.concatenate([held, outer], axis=0), preferred_element_type=F32)
        acc = p if g == 1 else acc + p
        if g == 7:
            store(acc, offset, total, i)


def store(acc, offset, total, i):
    for e in range(2):
        total[2 * i + e] = acc[:, e * 128 : (e + 1) * 128] + offset[...]


def project_half(first_half, w_out, offset, total):
    for i in range(4):
        for g in range(0, 8, 2):
            w = jnp.concatenate([w_out[g, :, 0:128], w_out[g + 1, :, 0:128]], axis=1)
            x = first_half[i, g : g + 2].reshape(256, 256)
            p = jnp.dot(w, x, preferred_element_type=F32)
            acc = p if g == 0 else acc + p
        store(acc, offset, total, i)


def unorder(total, maps, rows):
    x = total[...].reshape(384, 128)
    x0 = x.astype(BF16)
    r = x - x0.astype(F32)
    x1 = r.astype(BF16)
    x2 = (r - x1.astype(F32)).astype(BF16)
    y = [jnp.dot(part, maps[:, 768:896], preferred_element_type=F32) for part in (x0, x1, x2)]
    rows[...] = y[0] + (y[1] + y[2])


def picture(rows, o, f):
    return rows[pl.ds(o * 16 + f, 8, stride=48), :]


def own_kernel(
    hot, own, rim, queue, gain, w_in, w_mid, maps, spatial, lifted, inputs, act0, act1
):
    base = lift(hot, queue, maps)
    lifted[...] = base

    def frame(f):
        noisy = [own[ch, f + 8].astype(F32) for ch in range(3)]
        edge = [rim[ch, f + 8].astype(F32) for ch in range(3)]
        return tiles_of(noisy, edge, base[f * 8 + 64 : f * 8 + 72])

    network(inputs, 4, frame, maps, w_in, w_mid, gains(gain), act0, act1, spatial)


def late_kernel(
    offset, ahead, lifted, gain, w_in, w_mid, maps, w_mix, w_out, own,
    send, kept, inputs, act0, act1, spatial, total, rows,
):
    def frame(f):
        x = [ahead[ch, f].astype(F32) for ch in range(3)]
        noisy, edge = [tile[:8] for tile in x], [tile[8:] for tile in x]
        return tiles_of(noisy, edge, lifted[f * 8 + 128 : f * 8 + 136, :])

    network(inputs, 4, frame, maps, w_in, w_mid, gains(gain), act0, act1, spatial)
    predict([(own, 0), (spatial, 0)], w_mix, w_out, offset, total, kept)
    unorder(total, maps, rows)
    for f in range(8):
        w = ahead[0, f].astype(F32)
        share = w[15:16] / jnp.maximum(w[14:15] + w[15:16], 1.0)
        for o in range(3):
            send[o, f] = (picture(rows, o, f + 8) * share).astype(BF16)


def early_kernel(
    offset, shares, frames, rim, lifted, gain, w_in, w_mid, maps, w_mix, w_out, own, kept,
    mine, inputs, act0, act1, spatial, total, rows, total_next, rows_next,
):
    def frame(f):
        noisy = [frames[ch, f].astype(F32) for ch in range(3)]
        edge = [rim[ch, f].astype(F32) for ch in range(3)]
        return tiles_of(noisy, edge, lifted[f * 8 : f * 8 + 8, :])

    network(inputs, 4, frame, maps, w_in, w_mid, gains(gain), act0, act1, spatial)
    project_half(kept, w_out, offset, total_next)
    unorder(total_next, maps, rows_next)
    predict([(spatial, 0), (own, 0)], w_mix, w_out, offset, total)
    unorder(total, maps, rows)
    for f in range(16):
        lead, trail = shares[f : f + 1, :], shares[f + 16 : f + 17, :]
        for o in range(3):
            if f < 8:
                mine[o, f] = picture(rows, o, f) * lead
            else:
                mine[o, f] = picture(rows_next, o, f - 8) * lead + picture(rows, o, f) * trail


def join_kernel(mine, arrived, out):
    out[:, 0:8] = mine[:, 0:8] + arrived[...].astype(F32)
    out[:, 8:16] = mine[:, 8:16]


def network_scratch(frames):
    act = pltpu.VMEM((2, 10, 10, 16, 128), BF16)
    return [pltpu.VMEM((frames, 256, 128), BF16), act, act]


PICTURES = [pltpu.VMEM((8, 48, 128), F32), pltpu.VMEM((384, 128), F32)]


def shape(dims, kind):
    return jax.ShapeDtypeStruct(dims, kind)


def call(kernel, name, scalars, arrays, outs, scratch_shapes=(), flops=10**8, space=VMEM):
    if space is HBM:
        arrays = [pltpu.with_memory_space_constraint(a, pltpu.HBM) for a in arrays]
    return pl.pallas_call(
        kernel,
        out_shape=outs,
        in_specs=[SMEM] * len(scalars) + [space] * len(arrays),
        out_specs=tuple(VMEM for _ in outs),
        scratch_shapes=list(scratch_shapes),
        compiler_params=PARAMS,
        cost_estimate=pl.CostEstimate(flops=flops, bytes_accessed=10**6, transcendentals=0),
        name=name,
    )(*scalars, *arrays)


def copies_of(arrays):
    return [pltpu.VMEM(a.shape, a.dtype) for a in arrays] + [pltpu.SemaphoreType.DMA((len(arrays),))]


def body(
    noisy_frames, base_queue, frame_slot, blend_weight, weight_in, bias_in, gain_mid, weight_mid,
    time_mix, weight_out, bias_out,
):
    n_t = lax.axis_size("tm")
    n_r = lax.axis_size("rows")
    near = [(i, i ^ 1) for i in range(n_r)]
    far = [(i, (i - 1 ^ 1) + 1) for i in range(1, n_r - 1)]
    back = [(i + 1, i) for i in range(n_t - 1)]
    forth = [(i, i + 1) for i in range(n_t - 1)]
    blend = blend_weight.T
    tile = shape((3, 16, 8, 128), BF16)

    raw = [noisy_frames, jnp.transpose(base_queue[:, :, 0, :], (1, 0, 2))]
    to_near, to_far, base, own = call(
        pack_kernel,
        "pack",
        [],
        raw,
        (shape((144, 128), BF16), shape((144, 128), BF16), shape((48, 128), BF16), tile),
        [pltpu.VMEM((384, 128), F32)] + copies_of(raw)[1:],
        space=HBM,
    )
    from_far = lax.ppermute(to_far, "rows", far)
    from_near = lax.ppermute(to_near, "rows", near)
    raw = [
        jnp.asarray(tap_matrix(), BF16),
        weight_in.reshape(9, 6, 128),
        bias_in.reshape(1, 128),
        weight_mid.reshape(9, 128, 128),
        jnp.transpose(time_mix, (1, 2, 0)),
        weight_out.T,
        jnp.asarray(spread_matrix(), BF16),
        blend,
        frame_slot,
        bias_out,
    ]
    w_in, w_mid, w_mix, w_out, maps, weights, shares, hot, offset = call(
        prepare_kernel,
        "prepare",
        [],
        raw,
        (
            shape((5, 256, 256), BF16),
            shape((256, 1536), BF16),
            shape((8, 256, 256), BF16),
            shape((8, 48, 256), BF16),
            shape((128, 896), BF16),
            shape((16, 128), F32),
            shape((32, 128), F32),
            shape((192, 384), BF16),
            shape((48, 128), F32),
        ),
        copies_of(raw[:7])[:7]
        + [pltpu.SMEM(a.shape, a.dtype) for a in raw[7:]]
        + [pltpu.SemaphoreType.DMA((10,))],
        flops=2 * 10**9,
        space=HBM,
    )
    rim, ask, pack = pl.pallas_call(
        middle_kernel,
        out_shape=(tile, shape((n_t, 24, 128), BF16), shape((3, 8, 16, 128), BF16)),
        in_specs=[VMEM] * 5,
        out_specs=(VMEM,) * 3,
        scratch_shapes=[pltpu.VMEM((384, 128), F32)],
        compiler_params=PARAMS,
        name="middle",
    )(own, from_near, from_far, base, weights)
    queue = lax.all_to_all(ask, "tm", 0, 0, tiled=True)
    ahead = lax.ppermute(pack, "tm", back)
    gain = gain_mid.reshape(1, 128)
    spatial, lifted = call(
        own_kernel,
        "own",
        [],
        [hot, own, rim, queue, gain, w_in, w_mid, maps],
        (shape((4, 8, 128, 256), BF16), shape((192, 384), F32)),
        network_scratch(8),
        flops=10**10,
    )
    send, kept = call(
        late_kernel,
        "late",
        [],
        [offset, ahead, lifted, gain, w_in, w_mid, maps, w_mix, w_out, spatial],
        (shape((3, 8, 8, 128), BF16), shape((4, 8, 128, 256), BF16)),
        network_scratch(8) + [pltpu.VMEM((4, 8, 128, 256), BF16)] + PICTURES,
        flops=10**10,
    )
    arrived = lax.ppermute(send, "tm", forth)
    (mine,) = call(
        early_kernel,
        "early",
        [],
        [offset, shares, own, rim, lifted, gain, w_in, w_mid, maps, w_mix, w_out, spatial, kept],
        (shape((3, 16, 8, 128), F32),),
        network_scratch(8) + [pltpu.VMEM((4, 8, 128, 256), BF16)] + PICTURES + PICTURES,
        flops=10**10,
    )
    (out,) = call(join_kernel, "join", [], [mine, arrived], (shape((3, 16, 8, 128), F32),))
    return out


def solution(mesh):
    return jax.shard_map(
        body,
        mesh=mesh,
        in_specs=(
            P(None, "tm", "rows", None),
            P("tm", None, "rows", None),
            P(),
            P("tm", None),
            P(),
            P(),
            P(),
            P(),
            P(),
            P(),
            P(),
        ),
        out_specs=P(None, "tm", "rows", None),
        check_vma=False,
    )
```
